32 devices in a mesh: row: 16 (over z, x, core), col: 2 (over y).
Axes of the slice: x: 2, y: 2, z: 4, core: 2. Of those that a mesh axis runs over, the one named last changes fastest.
Arguments:
- eig_slab: float32 [8192, 4096], P('row', 'col'), may hold values from -6 to 6
- reflectors: float32 [16, 8192], P('col', 'row'), may hold values from -6 to 6
- row_offsets: int32 [16], replicated, may hold values from 1 to 24, as said below
Outputs:
- rotated: float32 [8192, 4096], P('row', 'col')
The draws below stay inside these ranges and needn't reach their ends.
Inputs may be any that keep to these rules, and one draw needn't show every extreme that they name: row_offsets[0] is 1; each next one is 1 or 2 larger than the one before, and exactly 8 of these steps are 2.
All inputs are finite; a program needn't handle non-finite values.
Results may differ from the reference program's by a relative error of at most 0.00027.
Values sent between devices are 32-bit elements; how exact they have to be, the bound alone decides.
No kernel may reach another device: no remote copies, remote signals or barrier semaphores. Data moves between devices by JAX's collectives and lax.ppermute only.
A program may use at most 64 MiB of HBM per device.

```python
import math
import jax
import jax.numpy as jnp
from jax import lax

NCOLS = 4096
WIDTH = 64
SWEEPS = 16
NROWS = 8192


def shared_offsets(key):
    order_key = jax.random.fold_in(key, 7)
    order = jax.random.permutation(order_key, SWEEPS - 1)
    steps_up = 1 + (order < SWEEPS // 2).astype(jnp.int32)
    later = 1 + jnp.cumsum(steps_up).astype(jnp.int32)
    return jnp.concatenate([jnp.ones((1,), jnp.int32), later]).astype(jnp.int32)


def draw_row_offsets(key, part):
    return shared_offsets(key)


def draw_reflectors(key, part):
    offsets = shared_offsets(key)
    key = jax.random.fold_in(key, 11)
    values = jnp.clip(jax.random.normal(key, (SWEEPS, NROWS), jnp.float32), -6.0, 6.0)
    rows_all = jnp.arange(NROWS, dtype=jnp.int32)
    phase = jnp.mod(rows_all[None, :] - offsets[:, None], WIDTH)
    heavy = (phase <= 1) | (phase >= WIDTH - 2)
    weights = jnp.where(heavy, jnp.float32(1.0), jnp.float32(0.02))
    return (values * weights).astype(jnp.float32)


def block_levels(rng, shape, split, smallest, high):
    factor_of = 1.0
    for position, blocks in split:
        heights = jax.random.uniform(jax.random.fold_in(jax.random.fold_in(rng, 6), position), (blocks,), jnp.float32, smallest / len(split), high / len(split))
        factor_of = factor_of * jnp.repeat(jnp.exp(heights), shape[position] // blocks).reshape((-1,) + (1,) * (len(shape) - 1 - position))
    return factor_of


def scatter_about(own_key, extent, deviation, most, pieces=(), kind=jnp.bfloat16):
    gain = block_levels(own_key, extent, pieces, -0.22, 0.18) if pieces else 1.0
    values = jax.random.normal(own_key, extent, jnp.float32) * deviation * gain
    return jnp.minimum(jnp.maximum(values, -most), most).astype(kind)


def setup_inputs(seed: int = 0) -> dict:
    key_list = jax.random.split(jax.random.key(seed), 4)
    eig_slab = scatter_about(key_list[0], (NROWS, NCOLS), 1.0, 6.0, ((0, 16), (1, 2)), jnp.float32)
    reflectors = draw_reflectors(jax.random.fold_in(key_list[3], 71), 0)
    row_offsets = draw_row_offsets(jax.random.fold_in(key_list[3], 71), 0)
    return dict(eig_slab=eig_slab, reflectors=reflectors, row_offsets=row_offsets)


def apply_sweep(eig_rows, eigen_columns, first_row, row_displacement, row_count_total, band_width):
    length, columns = eig_rows.shape
    overall_row_span = first_row + jnp.arange(length, dtype=jnp.int32)
    active_flags = (overall_row_span >= row_displacement) & (overall_row_span < row_count_total)
    eigen_columns = jnp.where(active_flags, eigen_columns, jnp.float32(0.0))
    shift = jnp.mod(row_displacement - first_row, band_width).astype(jnp.int32)
    zero_rows = jnp.zeros((band_width, columns), eig_rows.dtype)
    padded = jnp.concatenate([zero_rows, eig_rows, zero_rows], axis=0)
    zero_vec = jnp.zeros((band_width,), eigen_columns.dtype)
    padded_vec = jnp.concatenate([zero_vec, eigen_columns, zero_vec])
    integer_nought = jnp.zeros((band_width,), jnp.int32)
    extended_active_flags = jnp.concatenate([integer_nought, active_flags.astype(jnp.int32), integer_nought])
    windows_count = (length + band_width) // band_width
    windows = lax.dynamic_slice_in_dim(padded, shift, length + band_width, 0).reshape(windows_count, band_width, columns)
    window_vecs = lax.dynamic_slice_in_dim(padded_vec, shift, length + band_width, 0).reshape(windows_count, band_width)
    live_count = jnp.sum(lax.dynamic_slice_in_dim(extended_active_flags, shift, length + band_width, 0).reshape(windows_count, band_width), axis=1)
    squares = jnp.sum(window_vecs * window_vecs, axis=1)
    factor = jnp.where(live_count > 0, 2.0 / (squares + (live_count == 0).astype(jnp.float32)), jnp.float32(0.0))
    project = jnp.einsum("wr,wrc->wc", window_vecs, windows, precision=lax.Precision.HIGHEST)
    updated = windows - (factor[:, None] * window_vecs)[:, :, None] * project[:, None, :]
    padded = lax.dynamic_update_slice_in_dim(padded, updated.reshape(length + band_width, columns), shift, 0)
    return padded[band_width:band_width + length]


def reference(eig_slab, reflectors, row_offsets):
    col_block = math.gcd(NCOLS, 512)
    blocks = eig_slab.reshape(NROWS, NCOLS // col_block, col_block).transpose(1, 0, 2)

    def one_block(block_rows):
        for sweep_index in range(SWEEPS):
            block_rows = apply_sweep(block_rows, reflectors[sweep_index], 0, row_offsets[sweep_index], NROWS, WIDTH)
        return block_rows

    result = lax.map(one_block, blocks)
    return result.transpose(1, 0, 2).reshape(NROWS, NCOLS)
```

```python
import functools

import jax
import jax.numpy as jnp
from jax import lax
from jax.experimental import pallas as pl
from jax.experimental.pallas import tpu as pltpu
from jax.sharding import PartitionSpec as P

WIDTH = 64
SWEEPS = 16
WINDOWS = 8
ROWS = WIDTH * WINDOWS
HALF = ROWS // 2
BAND = 5 * SWEEPS
LOCAL = 7 * SWEEPS
EXTRA = 128
F32 = jnp.float32
BF16 = jnp.bfloat16


def split(a):
    hi = a.astype(BF16)
    return hi, (a - hi.astype(F32)).astype(BF16)


def mm(a, b):
    return jnp.dot(a, b, preferred_element_type=F32)


def mm_nt(a, b):
    return lax.dot_general(a, b, (((1,), (1,)), ((), ())), preferred_element_type=F32)


def mm3(a, b):
    return mm(a[0], b[0]) + mm(a[1], b[0]) + mm(a[0], b[1])


def iota(shape, dim):
    return lax.broadcasted_iota(jnp.int32, shape, dim)


def eliminate(target, column, row, first):
    if first < 7:
        return target - column * row
    lower = target[8:] - column[8:] * row
    return jnp.concatenate([target[:8], lower], axis=0)


def prepare_kernel(x_ref, off_ref, high_ref, low_ref, window_ref, xbuf, off, sems, off_sem):
    count = sems.shape[0]
    size = ROWS // count
    fetch = pltpu.make_async_copy(off_ref, off, off_sem)
    fetch.start()
    copies = []
    for j in range(count):
        rows = pl.ds(j * size, size)
        copies.append(pltpu.make_async_copy(x_ref.at[rows], xbuf.at[rows], sems.at[j]))
        copies[-1].start()
    fetch.wait()
    sweep = iota((SWEEPS, ROWS), 0)
    offset = jnp.zeros((SWEEPS, ROWS), jnp.int32)
    for s in range(SWEEPS):
        offset = jnp.where(sweep == s, off[s], offset)
    window = jnp.right_shift(iota((SWEEPS, ROWS), 1) - offset, 6)
    window_ref[...] = jnp.where((window < 0) & (lax.axis_index("row") == 0), -2, window)
    for j in range(count):
        copies[j].wait()
        rows = slice(j * size, (j + 1) * size)
        high, low = split(xbuf[rows])
        high_ref[rows] = high
        low_ref[rows] = low


def reflector_rows(vector_refs, window_ref):
    vectors = [ref[...] for ref in vector_refs]
    if len(vectors) == 2:
        first = lax.axis_index("col") == 0
        own, other = vectors
        vectors = [jnp.where(first, own, other), jnp.where(first, other, own)]
    refl = jnp.concatenate(vectors, axis=0)
    window = window_ref[...]
    return jnp.concatenate(
        [jnp.where(window == k, refl, 0.0) for k in range(-1, WINDOWS)], axis=0
    )


def halves_of(vt):
    return vt[:BAND, :HALF], vt[-BAND:, HALF:]


def project_kernel(chunk, inputs, *refs):
    window_ref, high_ref, low_ref = refs[inputs : inputs + 3]
    sums_ref, beside_ref, across_ref, down_ref, up_ref, solve_ref = refs[inputs + 3 :]
    columns = high_ref.shape[1]
    is_even = lax.rem(lax.axis_index("row"), 2) == 0
    vt = reflector_rows(refs[:inputs], window_ref)

    def send(cut, down, up):
        down_ref[:, cut] = down
        up_ref[:, cut] = up
        beside_ref[:, cut] = jnp.where(is_even, up[:8], down[:8])
        across_ref[:, cut] = jnp.where(is_even, down[:8], up[:8])

    tau = 2.0 / jnp.sum(vt[SWEEPS:-SWEEPS] * vt[SWEEPS:-SWEEPS], axis=1, keepdims=True)
    halves = [split(v) for v in halves_of(vt)]
    grams = [mm_nt(h, h) + mm_nt(l, h) + mm_nt(h, l) for h, l in halves]

    strict = iota((SWEEPS, BAND), 1) % SWEEPS < iota((SWEEPS, BAND), 0)

    def gram(k, shift):
        row = (k + 1) * SWEEPS
        if k < 3:
            return grams[0][row : row + SWEEPS], (k + 1 + shift) * SWEEPS
        row -= 4 * SWEEPS
        return grams[1][row : row + SWEEPS], (k - 3 + shift) * SWEEPS

    def strict_columns(k, shift, scale):
        block, base = gram(k, shift)
        if k == 3 and shift == 0:
            both = grams[0][4 * SWEEPS :, 4 * SWEEPS :] + grams[1][:SWEEPS, :SWEEPS]
            block, base = both, 0
        block = jnp.where(strict[:, : block.shape[1]], block, 0.0)
        if scale is not None:
            block = block * scale
        return lambda s: block[:, base + s : base + s + 1]

    tall = [jnp.concatenate([h, l], axis=0) for h, l in halves]
    chunks = columns // chunk

    def project(j):
        cut = slice(j * chunk, (j + 1) * chunk)
        sums = []
        for part in range(2):
            rows = slice(part * HALF, (part + 1) * HALF)
            both = mm(tall[part], high_ref[rows, cut])
            sums.append(both[:BAND] + both[BAND:] + mm(halves[part][0], low_ref[rows, cut]))
        shared = sums[0][-SWEEPS:] + sums[1][:SWEEPS]
        sums_ref[: 3 * SWEEPS, cut] = sums[0][SWEEPS:-SWEEPS]
        sums_ref[3 * SWEEPS : 4 * SWEEPS, cut] = shared
        sums_ref[4 * SWEEPS :, cut] = sums[1][SWEEPS:-SWEEPS]
        down_ref[:, cut] = sums[0][:SWEEPS]
        up_ref[:, cut] = sums[1][-SWEEPS:]

    lane = iota((SWEEPS, 128), 1)
    sub = iota((SWEEPS, 128), 0)
    state = []
    inner, outer = [], []
    for k in range(WINDOWS):
        here = lane == sub + k * SWEEPS
        if k < WINDOWS - 1:
            scale = tau[k * SWEEPS : (k + 1) * SWEEPS]
            state.append(jnp.where(here, scale, 0.0))
            inner.append(strict_columns(k, 0, scale))
            outer.append(strict_columns(k, 1, scale))
        else:
            state.append(jnp.where(here, 1.0, 0.0))
    leave = jnp.zeros((SWEEPS, 128), F32)
    leaving = strict_columns(-1, 1, None)
    for s in range(SWEEPS - 1):
        for j in range(s * chunks // (SWEEPS - 1), (s + 1) * chunks // (SWEEPS - 1)):
            project(j)
        rows = [state[k][s : s + 1] for k in range(WINDOWS)]
        for k in range(WINDOWS - 1):
            state[k] = eliminate(state[k], inner[k](s), rows[k], s)
            state[k] = eliminate(state[k], outer[k](s), rows[k + 1], s)
        leave = eliminate(leave, leaving(s), rows[0], s)

    solve = jnp.concatenate(state[: WINDOWS - 1], axis=0)
    solve_ref[...] = solve
    pass_on = split(leave[:, :LOCAL])

    bottom = jnp.concatenate([grams[0][:SWEEPS], jnp.zeros((SWEEPS, 128 - BAND), F32)], axis=1)
    top = jnp.concatenate([grams[1][-SWEEPS:], jnp.zeros((SWEEPS, 128 - BAND), F32)], axis=1)
    top = jnp.where(lane < SWEEPS, pltpu.roll(top, 128 - 4 * SWEEPS, 1), 0.0)
    response = pltpu.roll(leave, 2 * SWEEPS, 1)
    side = jnp.where(lane < SWEEPS, bottom, jnp.where(lane < 2 * SWEEPS, response, 0.0))
    send(slice(columns, columns + EXTRA), side, top)

    pass_tall = jnp.concatenate(pass_on, axis=0)
    for j in range(chunks):
        cut = slice(j * chunk, (j + 1) * chunk)
        high, low = split(sums_ref[:, cut])
        both = mm(pass_tall, high)
        leaving = both[:SWEEPS] + both[SWEEPS:] + mm(pass_on[0], low)
        send(cut, down_ref[:, cut] + leaving, up_ref[:, cut])


def bands_of(first, local, last):
    return (
        jnp.concatenate([first, local[: 4 * SWEEPS]], axis=0),
        jnp.concatenate([local[3 * SWEEPS :], last], axis=0),
    )


def stack(a):
    high, low = split(a)
    return jnp.concatenate([high, high, low], axis=0)


def straddling(gram, base):
    size = gram.shape[0]
    lane, sub = iota((size, 128), 1), iota((size, 128), 0)
    squares = jnp.sum(jnp.where(sub == lane, gram, 0.0), axis=1, keepdims=True)
    tau = jnp.where(squares > 0.0, 2.0 / squares, 0.0)
    strict = jnp.where(lane < sub, gram, 0.0) * tau
    return tau, strict, jnp.where(lane == sub + base, tau, 0.0)


def complete_kernel(parity, down_ref, up_ref, got_ref, *refs):
    send_refs = [ref for ref in refs if ref.shape[0] == 8]
    columns = down_ref.shape[1] - EXTRA
    row, count = lax.axis_index("row"), lax.axis_size("row")
    ours = lax.rem(row, 2) == parity

    def got(cut):
        return jnp.where(row < count - 1, got_ref[:, cut], 0.0)

    side = slice(columns, columns + EXTRA)
    own_side = down_ref[8:, side]
    _, strict, solve = straddling(up_ref[:8, side] + got(side), 0)
    carry = jnp.zeros((8, 128), F32)
    for s in range(8):
        row_s = solve[s : s + 1]
        carry = carry + own_side[:, SWEEPS + s : SWEEPS + s + 1] * row_s
        if s < 7:
            solve = solve - strict[:, s : s + 1] * row_s
    begin = 0
    for send_ref in send_refs:
        for place in range(0, send_ref.shape[1], 128):
            cut = slice(begin + place, begin + place + 128)
            down = down_ref[8:, cut]
            if cut.start < columns:
                below = up_ref[:8, cut] + got(cut)
                for s in range(8):
                    down = down + carry[:, s : s + 1] * below[s : s + 1]
            send_ref[:, place : place + 128] = jnp.where(ours, down, up_ref[8:, cut])
        begin += send_ref.shape[1]


def subtract_inside(chunk, begin, high_ref, low_ref, sums_ref, cols_ref, solve, inner_ref):
    solve = split(solve[:, :LOCAL])
    solve_tall = jnp.concatenate(solve, axis=0)
    none = jnp.zeros((SWEEPS, chunk), F32)
    for j in range(inner_ref.shape[1] // chunk):
        put = slice(j * chunk, (j + 1) * chunk)
        cut = slice(begin + j * chunk, begin + (j + 1) * chunk)
        high, low = split(sums_ref[:, cut])
        both = mm(solve_tall, high)
        coeff = both[:LOCAL] + both[LOCAL:] + mm(solve[0], low)
        for part, band in enumerate(bands_of(none, coeff, none)):
            rows = slice(part * HALF, (part + 1) * HALF)
            slab = high_ref[rows, cut].astype(F32) + low_ref[rows, cut].astype(F32)
            inner_ref[rows, put] = slab - mm(cols_ref[rows, :], stack(band))


def inside_kernel(chunk, inputs, *refs):
    window_ref, high_ref, low_ref, sums_ref, solve_ref, _ = refs[inputs : inputs + 6]
    inner_ref, ends_ref, cols_ref = refs[inputs + 6 :]
    for part, v in enumerate(halves_of(reflector_rows(refs[:inputs], window_ref))):
        high, low = (a.astype(F32) for a in split(v))
        tall = jnp.concatenate([high, low, high], axis=0)
        cols_ref[part * HALF : (part + 1) * HALF, :] = jnp.transpose(tall).astype(BF16)
    solve = solve_ref[...]
    lane = iota((LOCAL, 128), 1)
    spread = jnp.zeros((LOCAL, 128), F32)
    for group in range(3):
        begin = 2 * SWEEPS * group + SWEEPS
        moved = pltpu.roll(solve, SWEEPS + begin, 1)
        spread = jnp.where((lane >= begin) & (lane < begin + SWEEPS), moved, spread)
    lane, sub = iota((SWEEPS, 128), 1), iota((SWEEPS, 128), 0)
    used = lane < 6 * SWEEPS
    first = jnp.where((lane % (2 * SWEEPS) == sub) & used, 1.0, 0.0)
    last = jnp.where((lane % (2 * SWEEPS) == sub + SWEEPS) & used, 1.0, 0.0)
    for part, band in enumerate(bands_of(first, spread, last)):
        rows = slice(part * HALF, (part + 1) * HALF)
        high, low = split(mm(cols_ref[rows, :], stack(band)))
        group = iota((HALF, 128), 1) // (2 * SWEEPS)
        ends_ref[rows, :] = jnp.where(group == 1, low.astype(F32), high.astype(F32)).astype(BF16)

    subtract_inside(chunk, 0, high_ref, low_ref, sums_ref, cols_ref, solve, inner_ref)


def inside_more_kernel(chunk, high_ref, low_ref, sums_ref, solve_ref, cols_ref, inner_ref):
    begin = high_ref.shape[1] - inner_ref.shape[1]
    subtract_inside(chunk, begin, high_ref, low_ref, sums_ref, cols_ref, solve_ref[...], inner_ref)


def finish_kernel(chunk, *refs):
    across_refs, beside_refs, refs = refs[:2], refs[2:5], refs[5:]
    down_ref, up_ref, ends_ref = refs[:3]
    inner_refs, (out_ref, obuf, coeff_ref, sems) = refs[3:5], refs[5:]
    columns = 2 * inner_refs[0].shape[1]
    row, count = lax.axis_index("row"), lax.axis_size("row")
    is_even = lax.rem(row, 2) == 0

    def messages(cut):
        across = jnp.concatenate([ref[:, cut] for ref in across_refs], axis=0)
        across = jnp.where((row > 0) & (row < count - 1), across, 0.0)
        first, left, right = beside_refs
        middle = left.shape[1]
        if cut.start < middle:
            last = left[:, cut]
        else:
            last = right[:, cut.start - middle : cut.stop - middle]
        beside = jnp.concatenate([first[:, cut], last], axis=0)
        below = jnp.where(is_even, beside, across)
        above = jnp.where(is_even, across, beside)
        return down_ref[:, cut], up_ref[:, cut], below, above

    own_side, own_top, next_side, prev_top = messages(slice(columns, columns + EXTRA))
    _, n7, c7 = straddling(own_top + next_side, 0)
    tau1, n1, c1 = straddling(prev_top + own_side, SWEEPS)
    e1 = own_side * tau1
    for s in range(SWEEPS - 1):
        row7, row1 = c7[s : s + 1], c1[s : s + 1]
        c7 = eliminate(c7, n7[:, s : s + 1], row7, s)
        c1 = eliminate(c1, n1[:, s : s + 1], row1, s)
        c1 = eliminate(c1, -e1[:, SWEEPS + s : SWEEPS + s + 1], row7, s)
    join = split(jnp.concatenate([c1, c7], axis=0)[:, : 2 * SWEEPS])
    effect = ends_ref[:, : 6 * SWEEPS]

    for j in range(columns // chunk):
        cut = slice(j * chunk, (j + 1) * chunk)
        down, up, below, above = messages(cut)
        incoming = jnp.concatenate([up + below, down + above], axis=0)
        coeff_ref[:, cut] = stack(mm3(join, split(incoming)))

    stores = []
    for j in range(columns // chunk):
        cut = slice(j * chunk, (j + 1) * chunk)
        part, place = divmod(j * chunk, columns // 2)
        inner = inner_refs[part][:, place : place + chunk]
        obuf[:, cut] = inner - mm(effect, coeff_ref[:, cut])
        cut = pl.ds(j * chunk, chunk)
        stores.append(pltpu.make_async_copy(obuf.at[:, cut], out_ref.at[:, cut], sems.at[j]))
        stores[-1].start(priority=j % 2)
    for store in stores:
        store.wait()


def in_hbm(a):
    return pltpu.with_memory_space_constraint(a, pltpu.HBM)


def local(eig_slab, reflectors, row_offsets):
    rows, columns = eig_slab.shape
    assert rows == ROWS and columns % 256 == 0
    chunk = 256 if columns % 512 == 0 else 128
    chunks = columns // chunk
    count = lax.axis_size("row")
    groups = lax.axis_size("col")
    vmem = pl.BlockSpec(memory_space=pltpu.VMEM)
    hbm = pl.BlockSpec(memory_space=pltpu.HBM)
    params = pltpu.CompilerParams(vmem_limit_bytes=16 * 1024 * 1024)
    shape = jax.ShapeDtypeStruct
    slab_bytes = rows * columns * 4

    def cost(passes, flops):
        return pl.CostEstimate(flops=flops, bytes_accessed=passes * slab_bytes, transcendentals=0)

    if groups == 2:
        vectors = (reflectors, lax.ppermute(reflectors, "col", [(0, 1), (1, 0)]))
    elif groups == 1:
        vectors = (reflectors,)
    else:
        vectors = (lax.all_gather(reflectors, "col", axis=0, tiled=True),)

    high, low, window = pl.pallas_call(
        prepare_kernel,
        out_shape=(
            shape((rows, columns), BF16),
            shape((rows, columns), BF16),
            shape((SWEEPS, rows), jnp.int32),
        ),
        in_specs=[hbm, hbm],
        out_specs=(vmem,) * 3,
        scratch_shapes=[
            pltpu.VMEM((rows, columns), F32),
            pltpu.SMEM((SWEEPS,), jnp.int32),
            pltpu.SemaphoreType.DMA((8,)),
            pltpu.SemaphoreType.DMA(()),
        ],
        compiler_params=params,
        cost_estimate=cost(2, 0),
        name="prepare",
    )(in_hbm(eig_slab), in_hbm(row_offsets))

    own = shape((SWEEPS, columns + EXTRA), F32)
    eight = shape((8, columns + EXTRA), F32)
    sums, beside, across, down, up, solve = pl.pallas_call(
        functools.partial(project_kernel, chunk, len(vectors)),
        out_shape=(
            shape((LOCAL, columns), F32),
            eight,
            eight,
            own,
            own,
            shape((LOCAL, 128), F32),
        ),
        in_specs=[vmem] * (len(vectors) + 3),
        out_specs=(vmem,) * 6,
        compiler_params=params,
        cost_estimate=cost(2, rows * columns * 240),
        name="project",
    )(*vectors, window, high, low)

    pairs = [(i, i + 1) for i in range(0, count, 2)]
    on_chip = pairs + [(j, i) for i, j in pairs]
    pairs = [
        (i * groups + c, (i + 1) * groups + c)
        for i in range(1, count - 1, 2)
        for c in range(groups)
    ]
    pairs += [
        (i * groups + c, i * groups + c + 1)
        for i in (0, count - 1)
        for c in range(0, groups - 1, 2)
    ]
    over_chips = pairs + [(j, i) for i, j in pairs]

    got_beside = lax.ppermute(beside, "row", on_chip)
    got_across = lax.ppermute(across, ("row", "col"), over_chips)
    late = pl.pallas_call(
        functools.partial(complete_kernel, 0),
        out_shape=eight,
        in_specs=[vmem] * 3,
        out_specs=vmem,
        compiler_params=params,
        name="complete_even",
    )(down, up, got_beside)
    got_late = lax.ppermute(late, ("row", "col"), over_chips)

    half = shape((rows, columns // 2), F32)
    inner, ends, cols = pl.pallas_call(
        functools.partial(inside_kernel, chunk, len(vectors)),
        out_shape=(half, shape((rows, 128), BF16), shape((rows, 3 * BAND), BF16)),
        in_specs=[vmem] * (len(vectors) + 6),
        out_specs=(vmem,) * 3,
        compiler_params=params,
        cost_estimate=cost(2, rows * columns * 240),
        name="inside",
    )(*vectors, window, high, low, sums, solve, late)

    latest = pl.pallas_call(
        functools.partial(complete_kernel, 1),
        out_shape=(shape((8, columns // 2), F32), shape((8, columns // 2 + EXTRA), F32)),
        in_specs=[vmem] * 4,
        out_specs=(vmem,) * 2,
        compiler_params=params,
        name="complete_odd",
    )(down, up, got_across, ends)
    got_latest = [lax.ppermute(part, "row", on_chip) for part in latest]

    more = pl.pallas_call(
        functools.partial(inside_more_kernel, chunk),
        out_shape=half,
        in_specs=[vmem] * 5,
        out_specs=vmem,
        compiler_params=params,
        cost_estimate=cost(2, rows * columns * 240),
        name="inside_more",
    )(high, low, sums, solve, cols)

    return pl.pallas_call(
        functools.partial(finish_kernel, chunk),
        out_shape=shape((rows, columns), F32),
        in_specs=[vmem] * 10,
        out_specs=hbm,
        scratch_shapes=[
            pltpu.VMEM((rows, columns), F32),
            pltpu.VMEM((6 * SWEEPS, columns), BF16),
            pltpu.SemaphoreType.DMA((chunks,)),
        ],
        compiler_params=params,
        cost_estimate=cost(2, rows * columns * 200),
        name="finish",
    )(got_across, got_late, got_beside, *got_latest, down, up, ends, inner, more)


def solution(mesh):
    placed = (P("row", "col"), P("col", "row"), P())
    return jax.shard_map(
        local, mesh=mesh, in_specs=placed, out_specs=P("row", "col"), check_vma=False
    )
```

```python
import functools

import jax
import jax.numpy as jnp
from jax import lax
from jax.experimental import pallas as pl
from jax.experimental.pallas import tpu as pltpu
from jax.sharding import PartitionSpec as P

WIDTH = 64
SWEEPS = 16
WINDOWS = 8
ROWS = WIDTH * WINDOWS
HALF = ROWS // 2
BAND = 5 * SWEEPS
LOCAL = 7 * SWEEPS
EXTRA = 128
F32 = jnp.float32
BF16 = jnp.bfloat16


def split(a):
    hi = a.astype(BF16)
    return hi, (a - hi.astype(F32)).astype(BF16)


def mm(a, b):
    return jnp.dot(a, b, preferred_element_type=F32)


def mm_nt(a, b):
    return lax.dot_general(a, b, (((1,), (1,)), ((), ())), preferred_element_type=F32)


def mm3(a, b):
    return mm(a[0], b[0]) + mm(a[1], b[0]) + mm(a[0], b[1])


def left_pair(a):
    high, low = split(a)
    upper = jnp.concatenate([high, high], axis=1)
    lower = jnp.concatenate([low, jnp.zeros_like(low)], axis=1)
    return jnp.concatenate([upper, lower], axis=0)


def right_pair(a):
    high, low = split(a)
    none = jnp.zeros((128 - a.shape[0], a.shape[1]), BF16)
    return jnp.concatenate([high, none, low, none], axis=0)


def mm_pair(left, right):
    both = mm(left, right)
    half = left.shape[0] // 2
    return both[:half] + both[half:]


def iota(shape, dim):
    return lax.broadcasted_iota(jnp.int32, shape, dim)


def eliminate(target, column, row, first):
    if first < 7:
        return target - column * row
    lower = target[8:] - column[8:] * row
    return jnp.concatenate([target[:8], lower], axis=0)


def prepare_kernel(x_ref, off_ref, high_ref, low_ref, window_ref, xbuf, off, sems, off_sem):
    count = sems.shape[0]
    size = ROWS // count
    fetch = pltpu.make_async_copy(off_ref, off, off_sem)
    fetch.start()
    copies = []
    for j in range(count):
        rows = pl.ds(j * size, size)
        copies.append(pltpu.make_async_copy(x_ref.at[rows], xbuf.at[rows], sems.at[j]))
        copies[-1].start()
    fetch.wait()
    sweep = iota((SWEEPS, ROWS), 0)
    offset = jnp.zeros((SWEEPS, ROWS), jnp.int32)
    for s in range(SWEEPS):
        offset = jnp.where(sweep == s, off[s], offset)
    window = jnp.right_shift(iota((SWEEPS, ROWS), 1) - offset, 6)
    window_ref[...] = jnp.where((window < 0) & (lax.axis_index("row") == 0), -2, window)
    for j in range(count):
        copies[j].wait()
        rows = slice(j * size, (j + 1) * size)
        high, low = split(xbuf[rows])
        high_ref[rows] = high
        low_ref[rows] = low


def reflector_rows(vector_refs, window_ref):
    vectors = [ref[...] for ref in vector_refs]
    if len(vectors) == 2:
        first = lax.axis_index("col") == 0
        own, other = vectors
        vectors = [jnp.where(first, own, other), jnp.where(first, other, own)]
    refl = jnp.concatenate(vectors, axis=0)
    window = window_ref[...]
    return jnp.concatenate(
        [jnp.where(window == k, refl, 0.0) for k in range(-1, WINDOWS)], axis=0
    )


def halves_of(vt):
    return vt[:BAND, :HALF], vt[-BAND:, HALF:]


def project_kernel(chunk, inputs, *refs):
    window_ref, high_ref, low_ref = refs[inputs : inputs + 3]
    sums_ref, beside_ref, across_ref, down_ref, up_ref, solve_ref = refs[inputs + 3 :]
    columns = high_ref.shape[1]
    is_even = lax.rem(lax.axis_index("row"), 2) == 0
    vt = reflector_rows(refs[:inputs], window_ref)

    def send(cut, down, up):
        down_ref[:, cut] = down
        up_ref[:, cut] = up
        beside_ref[:, cut] = jnp.where(is_even, up[:8], down[:8])
        across_ref[:, cut] = jnp.where(is_even, down[:8], up[:8])

    tau = 2.0 / jnp.sum(vt[SWEEPS:-SWEEPS] * vt[SWEEPS:-SWEEPS], axis=1, keepdims=True)
    halves = [split(v) for v in halves_of(vt)]
    grams = [mm_nt(h, h) + mm_nt(l, h) + mm_nt(h, l) for h, l in halves]

    strict = iota((SWEEPS, BAND), 1) % SWEEPS < iota((SWEEPS, BAND), 0)

    def gram(k, shift):
        row = (k + 1) * SWEEPS
        if k < 3:
            return grams[0][row : row + SWEEPS], (k + 1 + shift) * SWEEPS
        row -= 4 * SWEEPS
        return grams[1][row : row + SWEEPS], (k - 3 + shift) * SWEEPS

    def strict_columns(k, shift, scale):
        block, base = gram(k, shift)
        if k == 3 and shift == 0:
            both = grams[0][4 * SWEEPS :, 4 * SWEEPS :] + grams[1][:SWEEPS, :SWEEPS]
            block, base = both, 0
        block = jnp.where(strict[:, : block.shape[1]], block, 0.0)
        if scale is not None:
            block = block * scale
        return lambda s: block[:, base + s : base + s + 1]

    tall = [jnp.concatenate([h, l], axis=0) for h, l in halves]
    chunks = columns // chunk

    def project(j):
        cut = slice(j * chunk, (j + 1) * chunk)
        sums = []
        for part in range(2):
            rows = slice(part * HALF, (part + 1) * HALF)
            both = mm(tall[part], high_ref[rows, cut])
            sums.append(both[:BAND] + both[BAND:] + mm(halves[part][0], low_ref[rows, cut]))
        shared = sums[0][-SWEEPS:] + sums[1][:SWEEPS]
        sums_ref[: 3 * SWEEPS, cut] = sums[0][SWEEPS:-SWEEPS]
        sums_ref[3 * SWEEPS : 4 * SWEEPS, cut] = shared
        sums_ref[4 * SWEEPS :, cut] = sums[1][SWEEPS:-SWEEPS]
        down_ref[:, cut] = sums[0][:SWEEPS]
        up_ref[:, cut] = sums[1][-SWEEPS:]

    lane = iota((SWEEPS, 128), 1)
    sub = iota((SWEEPS, 128), 0)
    state = []
    inner, outer = [], []
    for k in range(WINDOWS):
        here = lane == sub + k * SWEEPS
        if k < WINDOWS - 1:
            scale = tau[k * SWEEPS : (k + 1) * SWEEPS]
            state.append(jnp.where(here, scale, 0.0))
            inner.append(strict_columns(k, 0, scale))
            outer.append(strict_columns(k, 1, scale))
        else:
            state.append(jnp.where(here, 1.0, 0.0))
    leave = jnp.zeros((SWEEPS, 128), F32)
    leaving = strict_columns(-1, 1, None)
    for s in range(SWEEPS - 1):
        for j in range(s * chunks // (SWEEPS - 1), (s + 1) * chunks // (SWEEPS - 1)):
            project(j)
        rows = [state[k][s : s + 1] for k in range(WINDOWS)]
        for k in range(WINDOWS - 1):
            state[k] = eliminate(state[k], inner[k](s), rows[k], s)
            state[k] = eliminate(state[k], outer[k](s), rows[k + 1], s)
        leave = eliminate(leave, leaving(s), rows[0], s)

    solve = jnp.concatenate(state[: WINDOWS - 1], axis=0)
    solve_ref[...] = solve
    pass_on = left_pair(leave)

    bottom = jnp.concatenate([grams[0][:SWEEPS], jnp.zeros((SWEEPS, 128 - BAND), F32)], axis=1)
    top = jnp.concatenate([grams[1][-SWEEPS:], jnp.zeros((SWEEPS, 128 - BAND), F32)], axis=1)
    top = jnp.where(lane < SWEEPS, pltpu.roll(top, 128 - 4 * SWEEPS, 1), 0.0)
    response = pltpu.roll(leave, 2 * SWEEPS, 1)
    side = jnp.where(lane < SWEEPS, bottom, jnp.where(lane < 2 * SWEEPS, response, 0.0))
    extra = slice(columns, columns + EXTRA)
    down_ref[:, extra] = side
    up_ref[:, extra] = top

    def fold(a):
        return jnp.where(lane[:8] < SWEEPS, a[:8], pltpu.roll(a[8:], 2 * SWEEPS, 1))

    bottom, top = fold(bottom), fold(top)
    beside_ref[:, extra] = jnp.where(is_even, top, bottom)
    across_ref[:, extra] = jnp.where(is_even, bottom, top)

    for j in range(chunks):
        cut = slice(j * chunk, (j + 1) * chunk)
        leaving = mm_pair(pass_on, right_pair(sums_ref[:, cut]))
        send(cut, down_ref[:, cut] + leaving, up_ref[:, cut])


def bands_of(first, local, last):
    return (
        jnp.concatenate([first, local[: 4 * SWEEPS]], axis=0),
        jnp.concatenate([local[3 * SWEEPS :], last], axis=0),
    )


def stack(a):
    high, low = split(a)
    return jnp.concatenate([high, high, low], axis=0)


def straddling(gram, base):
    size = gram.shape[0]
    lane, sub = iota((size, 128), 1), iota((size, 128), 0)
    squares = jnp.sum(jnp.where(sub == lane, gram, 0.0), axis=1, keepdims=True)
    tau = jnp.where(squares > 0.0, 2.0 / squares, 0.0)
    strict = jnp.where(lane < sub, gram, 0.0) * tau
    return tau, strict, jnp.where(lane == sub + base, tau, 0.0)


def complete_kernel(parity, down_ref, up_ref, got_ref, *refs):
    send_ref = refs[-1]
    columns = down_ref.shape[1] - EXTRA
    row, count = lax.axis_index("row"), lax.axis_size("row")
    ours = lax.rem(row, 2) == parity

    def got(cut):
        return jnp.where(row < count - 1, got_ref[:, cut], 0.0)

    side = slice(columns, columns + EXTRA)
    own_side = down_ref[8:, side]
    _, strict, solve = straddling(up_ref[:8, side] + got(side), 0)
    carry = jnp.zeros((8, 128), F32)
    for s in range(8):
        row_s = solve[s : s + 1]
        carry = carry + own_side[:, SWEEPS + s : SWEEPS + s + 1] * row_s
        if s < 7:
            solve = solve - strict[:, s : s + 1] * row_s
    for place in range(0, columns, 128):
        cut = slice(place, place + 128)
        down = down_ref[8:, cut]
        below = up_ref[:8, cut] + got(cut)
        for s in range(8):
            down = down + carry[:, s : s + 1] * below[s : s + 1]
        send_ref[:, cut] = jnp.where(ours, down, up_ref[8:, cut])
    if send_ref.shape[1] > columns:
        send_ref[:, side] = jnp.zeros((8, EXTRA), F32)


def local_part(cut, high_ref, low_ref, sums_ref, cols_ref, solve):
    coeff = mm_pair(solve, right_pair(sums_ref[:, cut]))
    none = jnp.zeros((SWEEPS, coeff.shape[1]), F32)
    for part, band in enumerate(bands_of(none, coeff, none)):
        rows = slice(part * HALF, (part + 1) * HALF)
        slab = high_ref[rows, cut].astype(F32) + low_ref[rows, cut].astype(F32)
        yield rows, slab - mm(cols_ref[rows, :], stack(band))


def subtract_inside(chunk, begin, high_ref, low_ref, sums_ref, cols_ref, solve, inner_ref):
    solve = left_pair(solve)
    for place in range(0, inner_ref.shape[1], chunk):
        cut = slice(begin + place, begin + place + chunk)
        for rows, inner in local_part(cut, high_ref, low_ref, sums_ref, cols_ref, solve):
            inner_ref[rows, place : place + chunk] = inner


def inside_kernel(chunk, inputs, *refs):
    window_ref, high_ref, low_ref, sums_ref, solve_ref, _ = refs[inputs : inputs + 6]
    inner_ref, ends_ref, cols_ref = refs[inputs + 6 :]
    for part, v in enumerate(halves_of(reflector_rows(refs[:inputs], window_ref))):
        high, low = (a.astype(F32) for a in split(v))
        tall = jnp.concatenate([high, low, high], axis=0)
        cols_ref[part * HALF : (part + 1) * HALF, :] = jnp.transpose(tall).astype(BF16)
    solve = solve_ref[...]
    lane = iota((LOCAL, 128), 1)
    spread = jnp.zeros((LOCAL, 128), F32)
    for group in range(3):
        begin = 2 * SWEEPS * group + SWEEPS
        moved = pltpu.roll(solve, SWEEPS + begin, 1)
        spread = jnp.where((lane >= begin) & (lane < begin + SWEEPS), moved, spread)
    lane, sub = iota((SWEEPS, 128), 1), iota((SWEEPS, 128), 0)
    used = lane < 6 * SWEEPS
    first = jnp.where((lane % (2 * SWEEPS) == sub) & used, 1.0, 0.0)
    last = jnp.where((lane % (2 * SWEEPS) == sub + SWEEPS) & used, 1.0, 0.0)
    for part, band in enumerate(bands_of(first, spread, last)):
        rows = slice(part * HALF, (part + 1) * HALF)
        high, low = split(mm(cols_ref[rows, :], stack(band)))
        group = iota((HALF, 128), 1) // (2 * SWEEPS)
        ends_ref[rows, :] = jnp.where(group == 1, low.astype(F32), high.astype(F32)).astype(BF16)

    subtract_inside(chunk, 0, high_ref, low_ref, sums_ref, cols_ref, solve, inner_ref)


def from_neighbours(across, beside):
    row, count = lax.axis_index("row"), lax.axis_size("row")
    is_even = lax.rem(row, 2) == 0
    across = jnp.where((row > 0) & (row < count - 1), across, 0.0)
    return jnp.where(is_even, beside, across), jnp.where(is_even, across, beside)


def inside_more_kernel(chunk, begin, *refs):
    high_ref, low_ref, sums_ref, solve_ref, cols_ref = refs[:5]
    across_ref, beside_ref, down_ref, up_ref, ends_ref, inner_ref, effect_ref = refs[5:]
    extra = slice(down_ref.shape[1] - EXTRA, down_ref.shape[1])

    def unfold(a):
        return jnp.concatenate([a, pltpu.roll(a, 128 - 2 * SWEEPS, 1)], axis=0)

    below, above = from_neighbours(across_ref[:, extra], beside_ref[:, extra])
    own_side = down_ref[:, extra]
    _, n7, c7 = straddling(up_ref[:, extra] + unfold(below), 0)
    tau1, n1, c1 = straddling(unfold(above) + own_side, SWEEPS)
    e1 = own_side * tau1
    for s in range(SWEEPS - 1):
        row7, row1 = c7[s : s + 1], c1[s : s + 1]
        c7 = eliminate(c7, n7[:, s : s + 1], row7, s)
        c1 = eliminate(c1, n1[:, s : s + 1], row1, s)
        c1 = eliminate(c1, -e1[:, SWEEPS + s : SWEEPS + s + 1], row7, s)
    join = jnp.concatenate([c1, c7], axis=0)
    join = join + pltpu.roll(join, 2 * SWEEPS, 1) + pltpu.roll(join, 4 * SWEEPS, 1)
    high, low = split(mm(ends_ref[:, : 6 * SWEEPS], stack(join)))
    group = iota(high.shape, 1) // (2 * SWEEPS)
    effect = jnp.where(group == 1, low.astype(F32), high.astype(F32))
    effect_ref[...] = effect.astype(BF16)
    subtract_inside(chunk, begin, high_ref, low_ref, sums_ref, cols_ref, solve_ref[...], inner_ref)


def finish_kernel(chunk, *refs):
    first_across, last_across, first_beside, last_beside = refs[:4]
    down_ref, up_ref, effect_ref, high_ref, low_ref, sums_ref, cols_ref, solve_ref = refs[4:12]
    inner_refs, (out_ref, obuf, sems) = refs[12:14], refs[14:]
    columns = high_ref.shape[1]
    effect = effect_ref[:, : 6 * SWEEPS]
    solve = left_pair(solve_ref[...])

    def messages(cut):
        across = jnp.concatenate([first_across[:, cut], last_across[:, cut]], axis=0)
        beside = jnp.concatenate([first_beside[:, cut], last_beside[:, cut]], axis=0)
        below, above = from_neighbours(across, beside)
        return stack(jnp.concatenate([up_ref[:, cut] + below, down_ref[:, cut] + above], axis=0))

    stores = []
    pieces = []
    for ref in inner_refs:
        for place in range(0, ref.shape[1], chunk):
            pieces.append((ref, place))
    for j in range(columns // chunk):
        cut = slice(j * chunk, (j + 1) * chunk)
        coeff = messages(cut)
        if j < len(pieces):
            ref, place = pieces[j]
            obuf[:, cut] = ref[:, place : place + chunk] - mm(effect, coeff)
        else:
            for rows, inner in local_part(cut, high_ref, low_ref, sums_ref, cols_ref, solve):
                obuf[rows, cut] = inner - mm(effect[rows], coeff)
        cut = pl.ds(j * chunk, chunk)
        stores.append(pltpu.make_async_copy(obuf.at[:, cut], out_ref.at[:, cut], sems.at[j]))
        stores[-1].start()
    for store in stores:
        store.wait()


def in_hbm(a):
    return pltpu.with_memory_space_constraint(a, pltpu.HBM)


def local(eig_slab, reflectors, row_offsets):
    rows, columns = eig_slab.shape
    assert rows == ROWS and columns % 256 == 0
    chunk = 256 if columns % 512 == 0 else 128
    chunks = columns // chunk
    count = lax.axis_size("row")
    groups = lax.axis_size("col")
    vmem = pl.BlockSpec(memory_space=pltpu.VMEM)
    hbm = pl.BlockSpec(memory_space=pltpu.HBM)
    params = pltpu.CompilerParams(vmem_limit_bytes=16 * 1024 * 1024)
    shape = jax.ShapeDtypeStruct
    slab_bytes = rows * columns * 4

    def cost(passes, flops):
        return pl.CostEstimate(flops=flops, bytes_accessed=passes * slab_bytes, transcendentals=0)

    if groups == 2:
        vectors = (reflectors, lax.ppermute(reflectors, "col", [(0, 1), (1, 0)]))
    elif groups == 1:
        vectors = (reflectors,)
    else:
        vectors = (lax.all_gather(reflectors, "col", axis=0, tiled=True),)

    high, low, window = pl.pallas_call(
        prepare_kernel,
        out_shape=(
            shape((rows, columns), BF16),
            shape((rows, columns), BF16),
            shape((SWEEPS, rows), jnp.int32),
        ),
        in_specs=[hbm, hbm],
        out_specs=(vmem,) * 3,
        scratch_shapes=[
            pltpu.VMEM((rows, columns), F32),
            pltpu.SMEM((SWEEPS,), jnp.int32),
            pltpu.SemaphoreType.DMA((8,)),
            pltpu.SemaphoreType.DMA(()),
        ],
        compiler_params=params,
        cost_estimate=cost(2, 0),
        name="prepare",
    )(in_hbm(eig_slab), in_hbm(row_offsets))

    own = shape((SWEEPS, columns + EXTRA), F32)
    eight = shape((8, columns + EXTRA), F32)
    sums, beside, across, down, up, solve = pl.pallas_call(
        functools.partial(project_kernel, chunk, len(vectors)),
        out_shape=(
            shape((LOCAL, columns), F32),
            eight,
            eight,
            own,
            own,
            shape((LOCAL, 128), F32),
        ),
        in_specs=[vmem] * (len(vectors) + 3),
        out_specs=(vmem,) * 6,
        compiler_params=params,
        cost_estimate=cost(2, rows * columns * 240),
        name="project",
    )(*vectors, window, high, low)

    pairs = [(i, i + 1) for i in range(0, count, 2)]
    on_chip = pairs + [(j, i) for i, j in pairs]
    pairs = [
        (i * groups + c, (i + 1) * groups + c)
        for i in range(1, count - 1, 2)
        for c in range(groups)
    ]
    pairs += [
        (i * groups + c, i * groups + c + 1)
        for i in (0, count - 1)
        for c in range(0, groups - 1, 2)
    ]
    over_chips = pairs + [(j, i) for i, j in pairs]

    got_beside = lax.ppermute(beside, "row", on_chip)
    got_across = lax.ppermute(across, ("row", "col"), over_chips)
    late = pl.pallas_call(
        functools.partial(complete_kernel, 0),
        out_shape=eight,
        in_specs=[vmem] * 3,
        out_specs=vmem,
        compiler_params=params,
        name="complete_even",
    )(down, up, got_beside)
    got_late = lax.ppermute(late, ("row", "col"), over_chips)

    inside_first = (chunks + 1) // 2 * chunk
    inside_next = (chunks + 2) // 4 * chunk
    inner, ends, cols = pl.pallas_call(
        functools.partial(inside_kernel, chunk, len(vectors)),
        out_shape=(shape((rows, inside_first), F32), shape((rows, 128), BF16), shape((rows, 3 * BAND), BF16)),
        in_specs=[vmem] * (len(vectors) + 6),
        out_specs=(vmem,) * 3,
        compiler_params=params,
        cost_estimate=cost(2, rows * columns * 240),
        name="inside",
    )(*vectors, window, high, low, sums, solve, late)

    latest = pl.pallas_call(
        functools.partial(complete_kernel, 1),
        out_shape=shape((8, columns), F32),
        in_specs=[vmem] * 4,
        out_specs=vmem,
        compiler_params=params,
        name="complete_odd",
    )(down, up, got_across, ends)
    got_latest = lax.ppermute(latest, "row", on_chip)

    more, effect = pl.pallas_call(
        functools.partial(inside_more_kernel, chunk, inside_first),
        out_shape=(shape((rows, inside_next), F32), shape((rows, 128), BF16)),
        in_specs=[vmem] * 10,
        out_specs=(vmem,) * 2,
        compiler_params=params,
        cost_estimate=cost(2, rows * columns * 240),
        name="inside_more",
    )(high, low, sums, solve, cols, got_across, got_beside, down, up, ends)

    return pl.pallas_call(
        functools.partial(finish_kernel, chunk),
        out_shape=shape((rows, columns), F32),
        in_specs=[vmem] * 14,
        out_specs=hbm,
        scratch_shapes=[
            pltpu.VMEM((rows, columns), F32),
            pltpu.SemaphoreType.DMA((chunks,)),
        ],
        compiler_params=params,
        cost_estimate=cost(2, rows * columns * 200),
        name="finish",
    )(got_across, got_late, got_beside, got_latest, down, up, effect, high, low, sums, cols, solve, inner, more)


def solution(mesh):
    placed = (P("row", "col"), P("col", "row"), P())
    return jax.shard_map(
        local, mesh=mesh, in_specs=placed, out_specs=P("row", "col"), check_vma=False
    )
```

```python
import functools

import jax
import jax.numpy as jnp
from jax import lax
from jax.experimental import pallas as pl
from jax.experimental.pallas import tpu as pltpu
from jax.sharding import PartitionSpec as P

WIDTH = 64
SWEEPS = 16
WINDOWS = 8
ROWS = WIDTH * WINDOWS
HALF = ROWS // 2
BAND = 5 * SWEEPS
LOCAL = 7 * SWEEPS
EXTRA = 128
F32 = jnp.float32
BF16 = jnp.bfloat16


def split(a):
    hi = a.astype(BF16)
    return hi, (a - hi.astype(F32)).astype(BF16)


def mm(a, b):
    return jnp.dot(a, b, preferred_element_type=F32)


def mm_nt(a, b):
    return lax.dot_general(a, b, (((1,), (1,)), ((), ())), preferred_element_type=F32)


def mm3(a, b):
    return mm(a[0], b[0]) + mm(a[1], b[0]) + mm(a[0], b[1])


def left_pair(a):
    high, low = split(a)
    upper = jnp.concatenate([high, high], axis=1)
    lower = jnp.concatenate([low, jnp.zeros_like(low)], axis=1)
    return jnp.concatenate([upper, lower], axis=0)


def right_pair(a):
    high, low = split(a)
    none = jnp.zeros((128 - a.shape[0], a.shape[1]), BF16)
    return jnp.concatenate([high, none, low, none], axis=0)


def mm_pair(left, right):
    both = mm(left, right)
    half = left.shape[0] // 2
    return both[:half] + both[half:]


def iota(shape, dim):
    return lax.broadcasted_iota(jnp.int32, shape, dim)


def eliminate(target, column, row, first):
    if first < 7:
        return target - column * row
    lower = target[8:] - column[8:] * row
    return jnp.concatenate([target[:8], lower], axis=0)


def prepare_kernel(x_ref, off_ref, high_ref, low_ref, window_ref, xbuf, off, sems, off_sem):
    count = sems.shape[0]
    size = ROWS // count
    fetch = pltpu.make_async_copy(off_ref, off, off_sem)
    fetch.start()
    copies = []
    for j in range(count):
        rows = pl.ds(j * size, size)
        copies.append(pltpu.make_async_copy(x_ref.at[rows], xbuf.at[rows], sems.at[j]))
        copies[-1].start()
    fetch.wait()
    sweep = iota((SWEEPS, ROWS), 0)
    offset = jnp.zeros((SWEEPS, ROWS), jnp.int32)
    for s in range(SWEEPS):
        offset = jnp.where(sweep == s, off[s], offset)
    window = jnp.right_shift(iota((SWEEPS, ROWS), 1) - offset, 6)
    window_ref[...] = jnp.where((window < 0) & (lax.axis_index("row") == 0), -2, window)
    for j in range(count):
        copies[j].wait()
        rows = slice(j * size, (j + 1) * size)
        high, low = split(xbuf[rows])
        high_ref[rows] = high
        low_ref[rows] = low


def reflector_rows(vector_refs, window_ref):
    vectors = [ref[...] for ref in vector_refs]
    if len(vectors) == 2:
        first = lax.axis_index("col") == 0
        own, other = vectors
        vectors = [jnp.where(first, own, other), jnp.where(first, other, own)]
    refl = jnp.concatenate(vectors, axis=0)
    window = window_ref[...]
    return jnp.concatenate(
        [jnp.where(window == k, refl, 0.0) for k in range(-1, WINDOWS)], axis=0
    )


def halves_of(vt):
    return vt[:BAND, :HALF], vt[-BAND:, HALF:]


def project_kernel(chunk, inputs, *refs):
    window_ref, high_ref, low_ref = refs[inputs : inputs + 3]
    sums_ref, beside_ref, across_ref, down_ref, up_ref, solve_ref = refs[inputs + 3 :]
    columns = high_ref.shape[1]
    is_even = lax.rem(lax.axis_index("row"), 2) == 0
    vt = reflector_rows(refs[:inputs], window_ref)

    def send(cut, down, up):
        down_ref[:, cut] = down
        up_ref[:, cut] = up
        beside_ref[:, cut] = jnp.where(is_even, up[:8], down[:8])
        across_ref[:, cut] = jnp.where(is_even, down[:8], up[:8])

    tau = 2.0 / jnp.sum(vt[SWEEPS:-SWEEPS] * vt[SWEEPS:-SWEEPS], axis=1, keepdims=True)
    halves = [split(v) for v in halves_of(vt)]
    grams = [mm_nt(h, h) + mm_nt(l, h) + mm_nt(h, l) for h, l in halves]

    strict = iota((SWEEPS, BAND), 1) % SWEEPS < iota((SWEEPS, BAND), 0)

    def gram(k, shift):
        row = (k + 1) * SWEEPS
        if k < 3:
            return grams[0][row : row + SWEEPS], (k + 1 + shift) * SWEEPS
        row -= 4 * SWEEPS
        return grams[1][row : row + SWEEPS], (k - 3 + shift) * SWEEPS

    def strict_columns(k, shift, scale):
        block, base = gram(k, shift)
        if k == 3 and shift == 0:
            both = grams[0][4 * SWEEPS :, 4 * SWEEPS :] + grams[1][:SWEEPS, :SWEEPS]
            block, base = both, 0
        block = jnp.where(strict[:, : block.shape[1]], block, 0.0)
        if scale is not None:
            block = block * scale
        return lambda s: block[:, base + s : base + s + 1]

    tall = [jnp.concatenate([h, l], axis=0) for h, l in halves]
    chunks = columns // chunk

    def project(j):
        cut = slice(j * chunk, (j + 1) * chunk)
        sums = []
        for part in range(2):
            rows = slice(part * HALF, (part + 1) * HALF)
            both = mm(tall[part], high_ref[rows, cut])
            sums.append(both[:BAND] + both[BAND:] + mm(halves[part][0], low_ref[rows, cut]))
        shared = sums[0][-SWEEPS:] + sums[1][:SWEEPS]
        sums_ref[: 3 * SWEEPS, cut] = sums[0][SWEEPS:-SWEEPS]
        sums_ref[3 * SWEEPS : 4 * SWEEPS, cut] = shared
        sums_ref[4 * SWEEPS :, cut] = sums[1][SWEEPS:-SWEEPS]
        down_ref[:, cut] = sums[0][:SWEEPS]
        up_ref[:, cut] = sums[1][-SWEEPS:]

    lane = iota((SWEEPS, 128), 1)
    sub = iota((SWEEPS, 128), 0)
    state = []
    inner, outer = [], []
    for k in range(WINDOWS):
        here = lane == sub + k * SWEEPS
        if k < WINDOWS - 1:
            scale = tau[k * SWEEPS : (k + 1) * SWEEPS]
            state.append(jnp.where(here, scale, 0.0))
            inner.append(strict_columns(k, 0, scale))
            outer.append(strict_columns(k, 1, scale))
        else:
            state.append(jnp.where(here, 1.0, 0.0))
    leave = jnp.zeros((SWEEPS, 128), F32)
    leaving = strict_columns(-1, 1, None)
    for s in range(SWEEPS - 1):
        for j in range(s * chunks // (SWEEPS - 1), (s + 1) * chunks // (SWEEPS - 1)):
            project(j)
        rows = [state[k][s : s + 1] for k in range(WINDOWS)]
        for k in range(WINDOWS - 1):
            state[k] = eliminate(state[k], inner[k](s), rows[k], s)
            state[k] = eliminate(state[k], outer[k](s), rows[k + 1], s)
        leave = eliminate(leave, leaving(s), rows[0], s)

    solve = jnp.concatenate(state[: WINDOWS - 1], axis=0)
    solve_ref[...] = solve
    pass_on = left_pair(leave)

    bottom = jnp.concatenate([grams[0][:SWEEPS], jnp.zeros((SWEEPS, 128 - BAND), F32)], axis=1)
    top = jnp.concatenate([grams[1][-SWEEPS:], jnp.zeros((SWEEPS, 128 - BAND), F32)], axis=1)
    top = jnp.where(lane < SWEEPS, pltpu.roll(top, 128 - 4 * SWEEPS, 1), 0.0)
    response = pltpu.roll(leave, 2 * SWEEPS, 1)
    side = jnp.where(lane < SWEEPS, bottom, jnp.where(lane < 2 * SWEEPS, response, 0.0))
    extra = slice(columns, columns + EXTRA)
    down_ref[:, extra] = side
    up_ref[:, extra] = top

    def fold(a):
        return jnp.where(lane[:8] < SWEEPS, a[:8], pltpu.roll(a[8:], 2 * SWEEPS, 1))

    bottom, top = fold(bottom), fold(top)
    beside_ref[:, extra] = jnp.where(is_even, top, bottom)
    across_ref[:, extra] = jnp.where(is_even, bottom, top)

    for j in range(chunks):
        cut = slice(j * chunk, (j + 1) * chunk)
        leaving = mm_pair(pass_on, right_pair(sums_ref[:, cut]))
        send(cut, down_ref[:, cut] + leaving, up_ref[:, cut])


def bands_of(first, local, last):
    return (
        jnp.concatenate([first, local[: 4 * SWEEPS]], axis=0),
        jnp.concatenate([local[3 * SWEEPS :], last], axis=0),
    )


def stack(a):
    high, low = split(a)
    return jnp.concatenate([high, high, low], axis=0)


def straddling(gram, base):
    size = gram.shape[0]
    lane, sub = iota((size, 128), 1), iota((size, 128), 0)
    squares = jnp.sum(jnp.where(sub == lane, gram, 0.0), axis=1, keepdims=True)
    tau = jnp.where(squares > 0.0, 2.0 / squares, 0.0)
    strict = jnp.where(lane < sub, gram, 0.0) * tau
    return tau, strict, jnp.where(lane == sub + base, tau, 0.0)


def complete_kernel(parity, down_ref, up_ref, got_ref, *refs):
    send_ref = refs[-1]
    columns = down_ref.shape[1] - EXTRA
    row, count = lax.axis_index("row"), lax.axis_size("row")
    ours = lax.rem(row, 2) == parity

    def got(cut):
        return jnp.where(row < count - 1, got_ref[:, cut], 0.0)

    side = slice(columns, columns + EXTRA)
    own_side = down_ref[8:, side]
    _, strict, solve = straddling(up_ref[:8, side] + got(side), 0)
    carry = jnp.zeros((8, 128), F32)
    for s in range(8):
        row_s = solve[s : s + 1]
        carry = carry + own_side[:, SWEEPS + s : SWEEPS + s + 1] * row_s
        if s < 7:
            solve = solve - strict[:, s : s + 1] * row_s
    for place in range(0, columns, 128):
        cut = slice(place, place + 128)
        down = down_ref[8:, cut]
        below = up_ref[:8, cut] + got(cut)
        for s in range(8):
            down = down + carry[:, s : s + 1] * below[s : s + 1]
        send_ref[:, cut] = jnp.where(ours, down, up_ref[8:, cut])
    if send_ref.shape[1] > columns:
        send_ref[:, side] = jnp.zeros((8, EXTRA), F32)


def local_part(cut, high_ref, low_ref, sums_ref, cols_ref, solve):
    coeff = mm_pair(solve, right_pair(sums_ref[:, cut]))
    none = jnp.zeros((SWEEPS, coeff.shape[1]), F32)
    for part, band in enumerate(bands_of(none, coeff, none)):
        rows = slice(part * HALF, (part + 1) * HALF)
        slab = high_ref[rows, cut].astype(F32) + low_ref[rows, cut].astype(F32)
        yield rows, slab - mm(cols_ref[rows, :], stack(band))


def subtract_inside(chunk, begin, high_ref, low_ref, sums_ref, cols_ref, solve, inner_ref):
    solve = left_pair(solve)
    for place in range(0, inner_ref.shape[1], chunk):
        cut = slice(begin + place, begin + place + chunk)
        for rows, inner in local_part(cut, high_ref, low_ref, sums_ref, cols_ref, solve):
            inner_ref[rows, place : place + chunk] = inner


def inside_kernel(chunk, inputs, *refs):
    window_ref, high_ref, low_ref, sums_ref, solve_ref, _ = refs[inputs : inputs + 6]
    inner_ref, ends_ref, cols_ref = refs[inputs + 6 :]
    for part, v in enumerate(halves_of(reflector_rows(refs[:inputs], window_ref))):
        high, low = (a.astype(F32) for a in split(v))
        tall = jnp.concatenate([high, low, high], axis=0)
        cols_ref[part * HALF : (part + 1) * HALF, :] = jnp.transpose(tall).astype(BF16)
    solve = solve_ref[...]
    lane = iota((LOCAL, 128), 1)
    spread = jnp.zeros((LOCAL, 128), F32)
    for group in range(3):
        begin = 2 * SWEEPS * group + SWEEPS
        moved = pltpu.roll(solve, SWEEPS + begin, 1)
        spread = jnp.where((lane >= begin) & (lane < begin + SWEEPS), moved, spread)
    lane, sub = iota((SWEEPS, 128), 1), iota((SWEEPS, 128), 0)
    used = lane < 6 * SWEEPS
    first = jnp.where((lane % (2 * SWEEPS) == sub) & used, 1.0, 0.0)
    last = jnp.where((lane % (2 * SWEEPS) == sub + SWEEPS) & used, 1.0, 0.0)
    for part, band in enumerate(bands_of(first, spread, last)):
        rows = slice(part * HALF, (part + 1) * HALF)
        high, low = split(mm(cols_ref[rows, :], stack(band)))
        group = iota((HALF, 128), 1) // (2 * SWEEPS)
        ends_ref[rows, :] = jnp.where(group == 1, low.astype(F32), high.astype(F32)).astype(BF16)

    subtract_inside(chunk, 0, high_ref, low_ref, sums_ref, cols_ref, solve, inner_ref)


def from_neighbours(across, beside):
    row, count = lax.axis_index("row"), lax.axis_size("row")
    is_even = lax.rem(row, 2) == 0
    across = jnp.where((row > 0) & (row < count - 1), across, 0.0)
    return jnp.where(is_even, beside, across), jnp.where(is_even, across, beside)


def inside_more_kernel(chunk, begin, *refs):
    high_ref, low_ref, sums_ref, solve_ref, cols_ref = refs[:5]
    across_ref, beside_ref, down_ref, up_ref, ends_ref, inner_ref, effect_ref = refs[5:]
    extra = slice(down_ref.shape[1] - EXTRA, down_ref.shape[1])

    def unfold(a):
        return jnp.concatenate([a, pltpu.roll(a, 128 - 2 * SWEEPS, 1)], axis=0)

    below, above = from_neighbours(across_ref[:, extra], beside_ref[:, extra])
    own_side = down_ref[:, extra]
    _, n7, c7 = straddling(up_ref[:, extra] + unfold(below), 0)
    tau1, n1, c1 = straddling(unfold(above) + own_side, SWEEPS)
    e1 = own_side * tau1
    for s in range(SWEEPS - 1):
        row7, row1 = c7[s : s + 1], c1[s : s + 1]
        c7 = eliminate(c7, n7[:, s : s + 1], row7, s)
        c1 = eliminate(c1, n1[:, s : s + 1], row1, s)
        c1 = eliminate(c1, -e1[:, SWEEPS + s : SWEEPS + s + 1], row7, s)
    join = jnp.concatenate([c1, c7], axis=0)
    join = join + pltpu.roll(join, 2 * SWEEPS, 1) + pltpu.roll(join, 4 * SWEEPS, 1)
    high, low = split(mm(ends_ref[:, : 6 * SWEEPS], stack(join)))
    group = iota(high.shape, 1) // (2 * SWEEPS)
    effect = jnp.where(group == 1, low.astype(F32), high.astype(F32))
    effect_ref[...] = effect.astype(BF16)
    subtract_inside(chunk, begin, high_ref, low_ref, sums_ref, cols_ref, solve_ref[...], inner_ref)


def finish_kernel(chunk, *refs):
    first_across, last_across, first_beside, last_beside = refs[:4]
    down_ref, up_ref, effect_ref, high_ref, low_ref, sums_ref, cols_ref, solve_ref = refs[4:12]
    inner_refs, (out_ref, obuf, sems) = refs[12:14], refs[14:]
    columns = high_ref.shape[1]
    effect = effect_ref[:, : 6 * SWEEPS]
    solve = left_pair(solve_ref[...])

    def messages(cut):
        across = jnp.concatenate([first_across[:, cut], last_across[:, cut]], axis=0)
        beside = jnp.concatenate([first_beside[:, cut], last_beside[:, cut]], axis=0)
        below, above = from_neighbours(across, beside)
        return stack(jnp.concatenate([up_ref[:, cut] + below, down_ref[:, cut] + above], axis=0))

    stores = []
    pieces = []
    for ref in inner_refs:
        for place in range(0, ref.shape[1], chunk):
            pieces.append((ref, place))
    for j in range(columns // chunk):
        cut = slice(j * chunk, (j + 1) * chunk)
        coeff = messages(cut)
        if j < len(pieces):
            ref, place = pieces[j]
            obuf[:, cut] = ref[:, place : place + chunk] - mm(effect, coeff)
        else:
            for rows, inner in local_part(cut, high_ref, low_ref, sums_ref, cols_ref, solve):
                obuf[rows, cut] = inner - mm(effect[rows], coeff)
        cut = pl.ds(j * chunk, chunk)
        stores.append(pltpu.make_async_copy(obuf.at[:, cut], out_ref.at[:, cut], sems.at[j]))
        stores[-1].start()
    for store in stores:
        store.wait()


def in_hbm(a):
    return pltpu.with_memory_space_constraint(a, pltpu.HBM)


def local(eig_slab, reflectors, row_offsets):
    rows, columns = eig_slab.shape
    assert rows == ROWS and columns % 256 == 0
    chunk = 256 if columns % 512 == 0 else 128
    chunks = columns // chunk
    wide = 2 * chunk if chunks % 8 == 0 else chunk
    count = lax.axis_size("row")
    groups = lax.axis_size("col")
    vmem = pl.BlockSpec(memory_space=pltpu.VMEM)
    hbm = pl.BlockSpec(memory_space=pltpu.HBM)
    params = pltpu.CompilerParams(vmem_limit_bytes=16 * 1024 * 1024)
    shape = jax.ShapeDtypeStruct
    slab_bytes = rows * columns * 4

    def cost(passes, flops):
        return pl.CostEstimate(flops=flops, bytes_accessed=passes * slab_bytes, transcendentals=0)

    if groups == 2:
        vectors = (reflectors, lax.ppermute(reflectors, "col", [(0, 1), (1, 0)]))
    elif groups == 1:
        vectors = (reflectors,)
    else:
        vectors = (lax.all_gather(reflectors, "col", axis=0, tiled=True),)

    high, low, window = pl.pallas_call(
        prepare_kernel,
        out_shape=(
            shape((rows, columns), BF16),
            shape((rows, columns), BF16),
            shape((SWEEPS, rows), jnp.int32),
        ),
        in_specs=[hbm, hbm],
        out_specs=(vmem,) * 3,
        scratch_shapes=[
            pltpu.VMEM((rows, columns), F32),
            pltpu.SMEM((SWEEPS,), jnp.int32),
            pltpu.SemaphoreType.DMA((8,)),
            pltpu.SemaphoreType.DMA(()),
        ],
        compiler_params=params,
        cost_estimate=cost(2, 0),
        name="prepare",
    )(in_hbm(eig_slab), in_hbm(row_offsets))

    own = shape((SWEEPS, columns + EXTRA), F32)
    eight = shape((8, columns + EXTRA), F32)
    sums, beside, across, down, up, solve = pl.pallas_call(
        functools.partial(project_kernel, wide, len(vectors)),
        out_shape=(
            shape((LOCAL, columns), F32),
            eight,
            eight,
            own,
            own,
            shape((LOCAL, 128), F32),
        ),
        in_specs=[vmem] * (len(vectors) + 3),
        out_specs=(vmem,) * 6,
        compiler_params=params,
        cost_estimate=cost(2, rows * columns * 240),
        name="project",
    )(*vectors, window, high, low)

    pairs = [(i, i + 1) for i in range(0, count, 2)]
    on_chip = pairs + [(j, i) for i, j in pairs]
    pairs = [
        (i * groups + c, (i + 1) * groups + c)
        for i in range(1, count - 1, 2)
        for c in range(groups)
    ]
    pairs += [
        (i * groups + c, i * groups + c + 1)
        for i in (0, count - 1)
        for c in range(0, groups - 1, 2)
    ]
    over_chips = pairs + [(j, i) for i, j in pairs]

    got_beside = lax.ppermute(beside, "row", on_chip)
    got_across = lax.ppermute(across, ("row", "col"), over_chips)
    late = pl.pallas_call(
        functools.partial(complete_kernel, 0),
        out_shape=eight,
        in_specs=[vmem] * 3,
        out_specs=vmem,
        compiler_params=params,
        name="complete_even",
    )(down, up, got_beside)
    got_late = lax.ppermute(late, ("row", "col"), over_chips)

    inside_next = (chunks + 2) // 4 * chunk
    inside_first = columns - inside_next
    inner, ends, cols = pl.pallas_call(
        functools.partial(inside_kernel, wide, len(vectors)),
        out_shape=(shape((rows, inside_first), F32), shape((rows, 128), BF16), shape((rows, 3 * BAND), BF16)),
        in_specs=[vmem] * (len(vectors) + 6),
        out_specs=(vmem,) * 3,
        compiler_params=params,
        cost_estimate=cost(2, rows * columns * 240),
        name="inside",
    )(*vectors, window, high, low, sums, solve, late)

    latest = pl.pallas_call(
        functools.partial(complete_kernel, 1),
        out_shape=shape((8, columns), F32),
        in_specs=[vmem] * 4,
        out_specs=vmem,
        compiler_params=params,
        name="complete_odd",
    )(down, up, got_across, ends)
    got_latest = lax.ppermute(latest, "row", on_chip)

    more, effect = pl.pallas_call(
        functools.partial(inside_more_kernel, wide, inside_first),
        out_shape=(shape((rows, inside_next), F32), shape((rows, 128), BF16)),
        in_specs=[vmem] * 10,
        out_specs=(vmem,) * 2,
        compiler_params=params,
        cost_estimate=cost(2, rows * columns * 240),
        name="inside_more",
    )(high, low, sums, solve, cols, got_across, got_beside, down, up, ends)

    return pl.pallas_call(
        functools.partial(finish_kernel, chunk),
        out_shape=shape((rows, columns), F32),
        in_specs=[vmem] * 14,
        out_specs=hbm,
        scratch_shapes=[
            pltpu.VMEM((rows, columns), F32),
            pltpu.SemaphoreType.DMA((chunks,)),
        ],
        compiler_params=params,
        cost_estimate=cost(2, rows * columns * 200),
        name="finish",
    )(got_across, got_late, got_beside, got_latest, down, up, effect, high, low, sums, cols, solve, inner, more)


def solution(mesh):
    placed = (P("row", "col"), P("col", "row"), P())
    return jax.shard_map(
        local, mesh=mesh, in_specs=placed, out_specs=P("row", "col"), check_vma=False
    )
```

```python
import functools

import jax
import jax.numpy as jnp
from jax import lax
from jax.experimental import pallas as pl
from jax.experimental.pallas import tpu as pltpu
from jax.sharding import PartitionSpec as P

WIDTH = 64
SWEEPS = 16
WINDOWS = 8
ROWS = WIDTH * WINDOWS
HALF = ROWS // 2
BAND = 5 * SWEEPS
LOCAL = 7 * SWEEPS
EXTRA = 128
F32 = jnp.float32
BF16 = jnp.bfloat16


def split(a):
    hi = a.astype(BF16)
    return hi, (a - hi.astype(F32)).astype(BF16)


def mm(a, b):
    return jnp.dot(a, b, preferred_element_type=F32)


def mm_nt(a, b):
    return lax.dot_general(a, b, (((1,), (1,)), ((), ())), preferred_element_type=F32)


def mm3(a, b):
    return mm(a[0], b[0]) + mm(a[1], b[0]) + mm(a[0], b[1])


def left_pair(a):
    high, low = split(a)
    upper = jnp.concatenate([high, high], axis=1)
    lower = jnp.concatenate([low, jnp.zeros_like(low)], axis=1)
    return jnp.concatenate([upper, lower], axis=0)


def right_pair(a):
    high, low = split(a)
    none = jnp.zeros((128 - a.shape[0], a.shape[1]), BF16)
    return jnp.concatenate([high, none, low, none], axis=0)


def mm_pair(left, right):
    both = mm(left, right)
    half = left.shape[0] // 2
    return both[:half] + both[half:]


def iota(shape, dim):
    return lax.broadcasted_iota(jnp.int32, shape, dim)


def eliminate(target, column, row, first):
    if first < 7:
        return target - column * row
    lower = target[8:] - column[8:] * row
    return jnp.concatenate([target[:8], lower], axis=0)


def prepare_kernel(x_ref, off_ref, high_ref, low_ref, window_ref, xbuf, off, sems, off_sem):
    count = sems.shape[0]
    size = ROWS // count
    fetch = pltpu.make_async_copy(off_ref, off, off_sem)
    fetch.start()
    copies = []
    for j in range(count):
        rows = pl.ds(j * size, size)
        copies.append(pltpu.make_async_copy(x_ref.at[rows], xbuf.at[rows], sems.at[j]))
        copies[-1].start()
    fetch.wait()
    sweep = iota((SWEEPS, ROWS), 0)
    offset = jnp.zeros((SWEEPS, ROWS), jnp.int32)
    for s in range(SWEEPS):
        offset = jnp.where(sweep == s, off[s], offset)
    window = jnp.right_shift(iota((SWEEPS, ROWS), 1) - offset, 6)
    window_ref[...] = jnp.where((window < 0) & (lax.axis_index("row") == 0), -2, window)
    for j in range(count):
        copies[j].wait()
        rows = slice(j * size, (j + 1) * size)
        high, low = split(xbuf[rows])
        high_ref[rows] = high
        low_ref[rows] = low


def reflector_rows(vector_refs, window_ref):
    vectors = [ref[...] for ref in vector_refs]
    if len(vectors) == 2:
        first = lax.axis_index("col") == 0
        own, other = vectors
        vectors = [jnp.where(first, own, other), jnp.where(first, other, own)]
    refl = jnp.concatenate(vectors, axis=0)
    window = window_ref[...]
    return jnp.concatenate(
        [jnp.where(window == k, refl, 0.0) for k in range(-1, WINDOWS)], axis=0
    )


def halves_of(vt):
    return vt[:BAND, :HALF], vt[-BAND:, HALF:]


def project_kernel(chunk, inputs, *refs):
    window_ref, high_ref, low_ref = refs[inputs : inputs + 3]
    sums_ref, beside_ref, across_ref, down_ref, up_ref, solve_ref = refs[inputs + 3 :]
    columns = high_ref.shape[1]
    is_even = lax.rem(lax.axis_index("row"), 2) == 0
    vt = reflector_rows(refs[:inputs], window_ref)

    def send(cut, down, up):
        down_ref[:, cut] = down
        up_ref[:, cut] = up
        beside_ref[:, cut] = jnp.where(is_even, up[:8], down[:8])
        across_ref[:, cut] = jnp.where(is_even, down[:8], up[:8])

    tau = 2.0 / jnp.sum(vt[SWEEPS:-SWEEPS] * vt[SWEEPS:-SWEEPS], axis=1, keepdims=True)
    halves = [split(v) for v in halves_of(vt)]
    grams = [mm_nt(h, h) + mm_nt(l, h) + mm_nt(h, l) for h, l in halves]

    strict = iota((SWEEPS, BAND), 1) % SWEEPS < iota((SWEEPS, BAND), 0)

    def gram(k, shift):
        row = (k + 1) * SWEEPS
        if k < 3:
            return grams[0][row : row + SWEEPS], (k + 1 + shift) * SWEEPS
        row -= 4 * SWEEPS
        return grams[1][row : row + SWEEPS], (k - 3 + shift) * SWEEPS

    def strict_columns(k, shift, scale):
        block, base = gram(k, shift)
        if k == 3 and shift == 0:
            both = grams[0][4 * SWEEPS :, 4 * SWEEPS :] + grams[1][:SWEEPS, :SWEEPS]
            block, base = both, 0
        block = jnp.where(strict[:, : block.shape[1]], block, 0.0)
        if scale is not None:
            block = block * scale
        return lambda s: block[:, base + s : base + s + 1]

    tall = [jnp.concatenate([h, l], axis=0) for h, l in halves]
    chunks = columns // chunk

    def project(j):
        cut = slice(j * chunk, (j + 1) * chunk)
        sums = []
        for part in range(2):
            rows = slice(part * HALF, (part + 1) * HALF)
            both = mm(tall[part], high_ref[rows, cut])
            sums.append(both[:BAND] + both[BAND:] + mm(halves[part][0], low_ref[rows, cut]))
        shared = sums[0][-SWEEPS:] + sums[1][:SWEEPS]
        sums_ref[: 3 * SWEEPS, cut] = sums[0][SWEEPS:-SWEEPS]
        sums_ref[3 * SWEEPS : 4 * SWEEPS, cut] = shared
        sums_ref[4 * SWEEPS :, cut] = sums[1][SWEEPS:-SWEEPS]
        down_ref[:, cut] = sums[0][:SWEEPS]
        up_ref[:, cut] = sums[1][-SWEEPS:]

    lane = iota((SWEEPS, 128), 1)
    sub = iota((SWEEPS, 128), 0)
    state = []
    inner, outer = [], []
    for k in range(WINDOWS):
        here = lane == sub + k * SWEEPS
        if k < WINDOWS - 1:
            scale = tau[k * SWEEPS : (k + 1) * SWEEPS]
            state.append(jnp.where(here, scale, 0.0))
            inner.append(strict_columns(k, 0, scale))
            outer.append(strict_columns(k, 1, scale))
        else:
            state.append(jnp.where(here, 1.0, 0.0))
    leave = jnp.zeros((SWEEPS, 128), F32)
    leaving = strict_columns(-1, 1, None)
    for s in range(SWEEPS - 1):
        for j in range(s * chunks // (SWEEPS - 1), (s + 1) * chunks // (SWEEPS - 1)):
            project(j)
        rows = [state[k][s : s + 1] for k in range(WINDOWS)]
        for k in range(WINDOWS - 1):
            state[k] = eliminate(state[k], inner[k](s), rows[k], s)
            state[k] = eliminate(state[k], outer[k](s), rows[k + 1], s)
        leave = eliminate(leave, leaving(s), rows[0], s)

    solve = jnp.concatenate(state[: WINDOWS - 1], axis=0)
    solve_ref[...] = solve
    pass_on = left_pair(leave)

    bottom = jnp.concatenate([grams[0][:SWEEPS], jnp.zeros((SWEEPS, 128 - BAND), F32)], axis=1)
    top = jnp.concatenate([grams[1][-SWEEPS:], jnp.zeros((SWEEPS, 128 - BAND), F32)], axis=1)
    top = jnp.where(lane < SWEEPS, pltpu.roll(top, 128 - 4 * SWEEPS, 1), 0.0)
    response = pltpu.roll(leave, 2 * SWEEPS, 1)
    side = jnp.where(lane < SWEEPS, bottom, jnp.where(lane < 2 * SWEEPS, response, 0.0))
    extra = slice(columns, columns + EXTRA)
    down_ref[:, extra] = side
    up_ref[:, extra] = top

    def fold(a):
        return jnp.where(lane[:8] < SWEEPS, a[:8], pltpu.roll(a[8:], 2 * SWEEPS, 1))

    bottom, top = fold(bottom), fold(top)
    beside_ref[:, extra] = jnp.where(is_even, top, bottom)
    across_ref[:, extra] = jnp.where(is_even, bottom, top)

    for j in range(chunks):
        cut = slice(j * chunk, (j + 1) * chunk)
        leaving = mm_pair(pass_on, right_pair(sums_ref[:, cut]))
        send(cut, down_ref[:, cut] + leaving, up_ref[:, cut])


def bands_of(first, local, last):
    return (
        jnp.concatenate([first, local[: 4 * SWEEPS]], axis=0),
        jnp.concatenate([local[3 * SWEEPS :], last], axis=0),
    )


def stack(a):
    high, low = split(a)
    return jnp.concatenate([high, high, low], axis=0)


def straddling(gram, base):
    size = gram.shape[0]
    lane, sub = iota((size, 128), 1), iota((size, 128), 0)
    squares = jnp.sum(jnp.where(sub == lane, gram, 0.0), axis=1, keepdims=True)
    tau = jnp.where(squares > 0.0, 2.0 / squares, 0.0)
    strict = jnp.where(lane < sub, gram, 0.0) * tau
    return tau, strict, jnp.where(lane == sub + base, tau, 0.0)


def complete_kernel(parity, down_ref, up_ref, got_ref, *refs):
    send_ref = refs[-1]
    columns = down_ref.shape[1] - EXTRA
    row, count = lax.axis_index("row"), lax.axis_size("row")
    ours = lax.rem(row, 2) == parity

    def got(cut):
        return jnp.where(row < count - 1, got_ref[:, cut], 0.0)

    side = slice(columns, columns + EXTRA)
    own_side = down_ref[8:, side]
    _, strict, solve = straddling(up_ref[:8, side] + got(side), 0)
    carry = jnp.zeros((8, 128), F32)
    for s in range(8):
        row_s = solve[s : s + 1]
        carry = carry + own_side[:, SWEEPS + s : SWEEPS + s + 1] * row_s
        if s < 7:
            solve = solve - strict[:, s : s + 1] * row_s
    for place in range(0, columns, 128):
        cut = slice(place, place + 128)
        down = down_ref[8:, cut]
        below = up_ref[:8, cut] + got(cut)
        for s in range(8):
            down = down + carry[:, s : s + 1] * below[s : s + 1]
        send_ref[:, cut] = jnp.where(ours, down, up_ref[8:, cut])
    if send_ref.shape[1] > columns:
        send_ref[:, side] = jnp.zeros((8, EXTRA), F32)


def local_part(cut, high_ref, low_ref, sums_ref, cols_ref, solve):
    coeff = mm_pair(solve, right_pair(sums_ref[:, cut]))
    none = jnp.zeros((SWEEPS, coeff.shape[1]), F32)
    for part, band in enumerate(bands_of(none, coeff, none)):
        rows = slice(part * HALF, (part + 1) * HALF)
        slab = high_ref[rows, cut].astype(F32) + low_ref[rows, cut].astype(F32)
        yield rows, slab - mm(cols_ref[rows, :], stack(band))


def subtract_inside(chunk, begin, high_ref, low_ref, sums_ref, cols_ref, solve, inner_ref):
    solve = left_pair(solve)
    for place in range(0, inner_ref.shape[1], chunk):
        cut = slice(begin + place, begin + place + chunk)
        for rows, inner in local_part(cut, high_ref, low_ref, sums_ref, cols_ref, solve):
            inner_ref[rows, place : place + chunk] = inner


def inside_kernel(chunk, inputs, *refs):
    window_ref, high_ref, low_ref, sums_ref, solve_ref, _ = refs[inputs : inputs + 6]
    inner_ref, ends_ref, cols_ref = refs[inputs + 6 :]
    for part, v in enumerate(halves_of(reflector_rows(refs[:inputs], window_ref))):
        high, low = (a.astype(F32) for a in split(v))
        tall = jnp.concatenate([high, low, high], axis=0)
        cols_ref[part * HALF : (part + 1) * HALF, :] = jnp.transpose(tall).astype(BF16)
    solve = solve_ref[...]
    lane = iota((LOCAL, 128), 1)
    spread = jnp.zeros((LOCAL, 128), F32)
    for group in range(3):
        begin = 2 * SWEEPS * group + SWEEPS
        moved = pltpu.roll(solve, SWEEPS + begin, 1)
        spread = jnp.where((lane >= begin) & (lane < begin + SWEEPS), moved, spread)
    lane, sub = iota((SWEEPS, 128), 1), iota((SWEEPS, 128), 0)
    used = lane < 6 * SWEEPS
    first = jnp.where((lane % (2 * SWEEPS) == sub) & used, 1.0, 0.0)
    last = jnp.where((lane % (2 * SWEEPS) == sub + SWEEPS) & used, 1.0, 0.0)
    for part, band in enumerate(bands_of(first, spread, last)):
        rows = slice(part * HALF, (part + 1) * HALF)
        high, low = split(mm(cols_ref[rows, :], stack(band)))
        group = iota((HALF, 128), 1) // (2 * SWEEPS)
        ends_ref[rows, :] = jnp.where(group == 1, low.astype(F32), high.astype(F32)).astype(BF16)

    subtract_inside(chunk, 0, high_ref, low_ref, sums_ref, cols_ref, solve, inner_ref)


def from_neighbours(across, beside):
    row, count = lax.axis_index("row"), lax.axis_size("row")
    is_even = lax.rem(row, 2) == 0
    across = jnp.where((row > 0) & (row < count - 1), across, 0.0)
    return jnp.where(is_even, beside, across), jnp.where(is_even, across, beside)


def inside_more_kernel(chunk, begin, *refs):
    high_ref, low_ref, sums_ref, solve_ref, cols_ref = refs[:5]
    across_ref, beside_ref, down_ref, up_ref, ends_ref, inner_ref, effect_ref = refs[5:]
    extra = slice(down_ref.shape[1] - EXTRA, down_ref.shape[1])

    def unfold(a):
        return jnp.concatenate([a, pltpu.roll(a, 128 - 2 * SWEEPS, 1)], axis=0)

    below, above = from_neighbours(across_ref[:, extra], beside_ref[:, extra])
    own_side = down_ref[:, extra]
    _, n7, c7 = straddling(up_ref[:, extra] + unfold(below), 0)
    tau1, n1, c1 = straddling(unfold(above) + own_side, SWEEPS)
    e1 = own_side * tau1
    for s in range(SWEEPS - 1):
        row7, row1 = c7[s : s + 1], c1[s : s + 1]
        c7 = eliminate(c7, n7[:, s : s + 1], row7, s)
        c1 = eliminate(c1, n1[:, s : s + 1], row1, s)
        c1 = eliminate(c1, -e1[:, SWEEPS + s : SWEEPS + s + 1], row7, s)
    join = jnp.concatenate([c1, c7], axis=0)
    join = join + pltpu.roll(join, 2 * SWEEPS, 1) + pltpu.roll(join, 4 * SWEEPS, 1)
    high, low = split(mm(ends_ref[:, : 6 * SWEEPS], stack(join)))
    group = iota(high.shape, 1) // (2 * SWEEPS)
    effect = jnp.where(group == 1, low.astype(F32), high.astype(F32))
    effect_ref[...] = effect.astype(BF16)
    subtract_inside(chunk, begin, high_ref, low_ref, sums_ref, cols_ref, solve_ref[...], inner_ref)


def finish_kernel(chunk, *refs):
    first_across, last_across, first_beside, last_beside = refs[:4]
    down_ref, up_ref, effect_ref, high_ref, low_ref, sums_ref, cols_ref, solve_ref = refs[4:12]
    inner_refs, (out_ref, obuf, sems) = refs[12:14], refs[14:]
    columns = high_ref.shape[1]
    effect = effect_ref[:, : 6 * SWEEPS]
    solve = left_pair(solve_ref[...])

    def messages(cut):
        across = jnp.concatenate([first_across[:, cut], last_across[:, cut]], axis=0)
        beside = jnp.concatenate([first_beside[:, cut], last_beside[:, cut]], axis=0)
        below, above = from_neighbours(across, beside)
        return stack(jnp.concatenate([up_ref[:, cut] + below, down_ref[:, cut] + above], axis=0))

    cuts = []
    start = 0
    for ref in inner_refs:
        for place in range(0, ref.shape[1], chunk):
            cuts.append((start + place, chunk, ref, place))
        start += ref.shape[1]

    def halved(cut):
        begin, width, ref, place = cut
        width //= 2
        return [(begin, width, ref, place), (begin + width, width, ref, place + width)]

    if chunk == 256:
        cuts = halved(cuts[0]) + cuts[1:-1] + halved(cuts[-1])
    for at, begin in enumerate(range(start, columns, chunk)):
        cuts.insert(2 + 3 * at, (begin, chunk, None, 0))

    stores = []
    for j, (begin, width, ref, place) in enumerate(cuts):
        cut = slice(begin, begin + width)
        coeff = messages(cut)
        if ref is not None:
            obuf[:, cut] = ref[:, place : place + width] - mm(effect, coeff)
        else:
            for rows, inner in local_part(cut, high_ref, low_ref, sums_ref, cols_ref, solve):
                obuf[rows, cut] = inner - mm(effect[rows], coeff)
        cut = pl.ds(begin, width)
        stores.append(pltpu.make_async_copy(obuf.at[:, cut], out_ref.at[:, cut], sems.at[j]))
        stores[-1].start()
    for store in stores:
        store.wait()


def in_hbm(a):
    return pltpu.with_memory_space_constraint(a, pltpu.HBM)


def local(eig_slab, reflectors, row_offsets):
    rows, columns = eig_slab.shape
    assert rows == ROWS and columns % 256 == 0
    chunk = 256 if columns % 512 == 0 else 128
    chunks = columns // chunk
    count = lax.axis_size("row")
    groups = lax.axis_size("col")
    vmem = pl.BlockSpec(memory_space=pltpu.VMEM)
    hbm = pl.BlockSpec(memory_space=pltpu.HBM)
    params = pltpu.CompilerParams(vmem_limit_bytes=16 * 1024 * 1024)
    shape = jax.ShapeDtypeStruct
    slab_bytes = rows * columns * 4

    def cost(passes, flops):
        return pl.CostEstimate(flops=flops, bytes_accessed=passes * slab_bytes, transcendentals=0)

    if groups == 2:
        vectors = (reflectors, lax.ppermute(reflectors, "col", [(0, 1), (1, 0)]))
    elif groups == 1:
        vectors = (reflectors,)
    else:
        vectors = (lax.all_gather(reflectors, "col", axis=0, tiled=True),)

    high, low, window = pl.pallas_call(
        prepare_kernel,
        out_shape=(
            shape((rows, columns), BF16),
            shape((rows, columns), BF16),
            shape((SWEEPS, rows), jnp.int32),
        ),
        in_specs=[hbm, hbm],
        out_specs=(vmem,) * 3,
        scratch_shapes=[
            pltpu.VMEM((rows, columns), F32),
            pltpu.SMEM((SWEEPS,), jnp.int32),
            pltpu.SemaphoreType.DMA((8,)),
            pltpu.SemaphoreType.DMA(()),
        ],
        compiler_params=params,
        cost_estimate=cost(2, 0),
        name="prepare",
    )(in_hbm(eig_slab), in_hbm(row_offsets))

    own = shape((SWEEPS, columns + EXTRA), F32)
    eight = shape((8, columns + EXTRA), F32)
    sums, beside, across, down, up, solve = pl.pallas_call(
        functools.partial(project_kernel, chunk, len(vectors)),
        out_shape=(
            shape((LOCAL, columns), F32),
            eight,
            eight,
            own,
            own,
            shape((LOCAL, 128), F32),
        ),
        in_specs=[vmem] * (len(vectors) + 3),
        out_specs=(vmem,) * 6,
        compiler_params=params,
        cost_estimate=cost(2, rows * columns * 240),
        name="project",
    )(*vectors, window, high, low)

    pairs = [(i, i + 1) for i in range(0, count, 2)]
    on_chip = pairs + [(j, i) for i, j in pairs]
    pairs = [
        (i * groups + c, (i + 1) * groups + c)
        for i in range(1, count - 1, 2)
        for c in range(groups)
    ]
    pairs += [
        (i * groups + c, i * groups + c + 1)
        for i in (0, count - 1)
        for c in range(0, groups - 1, 2)
    ]
    over_chips = pairs + [(j, i) for i, j in pairs]

    got_beside = lax.ppermute(beside, "row", on_chip)
    got_across = lax.ppermute(across, ("row", "col"), over_chips)
    late = pl.pallas_call(
        functools.partial(complete_kernel, 0),
        out_shape=eight,
        in_specs=[vmem] * 3,
        out_specs=vmem,
        compiler_params=params,
        name="complete_even",
    )(down, up, got_beside)
    got_late = lax.ppermute(late, ("row", "col"), over_chips)

    inside_first = (chunks + 1) // 2 * chunk
    inside_next = (chunks + 2) // 4 * chunk
    inner, ends, cols = pl.pallas_call(
        functools.partial(inside_kernel, chunk, len(vectors)),
        out_shape=(shape((rows, inside_first), F32), shape((rows, 128), BF16), shape((rows, 3 * BAND), BF16)),
        in_specs=[vmem] * (len(vectors) + 6),
        out_specs=(vmem,) * 3,
        compiler_params=params,
        cost_estimate=cost(2, rows * columns * 240),
        name="inside",
    )(*vectors, window, high, low, sums, solve, late)

    latest = pl.pallas_call(
        functools.partial(complete_kernel, 1),
        out_shape=shape((8, columns), F32),
        in_specs=[vmem] * 4,
        out_specs=vmem,
        compiler_params=params,
        name="complete_odd",
    )(down, up, got_across, ends)
    got_latest = lax.ppermute(latest, "row", on_chip)

    more, effect = pl.pallas_call(
        functools.partial(inside_more_kernel, chunk, inside_first),
        out_shape=(shape((rows, inside_next), F32), shape((rows, 128), BF16)),
        in_specs=[vmem] * 10,
        out_specs=(vmem,) * 2,
        compiler_params=params,
        cost_estimate=cost(2, rows * columns * 240),
        name="inside_more",
    )(high, low, sums, solve, cols, got_across, got_beside, down, up, ends)

    return pl.pallas_call(
        functools.partial(finish_kernel, chunk),
        out_shape=shape((rows, columns), F32),
        in_specs=[vmem] * 14,
        out_specs=hbm,
        scratch_shapes=[
            pltpu.VMEM((rows, columns), F32),
            pltpu.SemaphoreType.DMA((chunks + 2,)),
        ],
        compiler_params=params,
        cost_estimate=cost(2, rows * columns * 200),
        name="finish",
    )(got_across, got_late, got_beside, got_latest, down, up, effect, high, low, sums, cols, solve, inner, more)


def solution(mesh):
    placed = (P("row", "col"), P("col", "row"), P())
    return jax.shard_map(
        local, mesh=mesh, in_specs=placed, out_specs=P("row", "col"), check_vma=False
    )
```

```python
import functools

import jax
import jax.numpy as jnp
from jax import lax
from jax.experimental import pallas as pl
from jax.experimental.pallas import tpu as pltpu
from jax.sharding import PartitionSpec as P

WIDTH = 64
SWEEPS = 16
WINDOWS = 8
ROWS = WIDTH * WINDOWS
HALF = ROWS // 2
BAND = 5 * SWEEPS
LOCAL = 7 * SWEEPS
EXTRA = 128
F32 = jnp.float32
BF16 = jnp.bfloat16


def split(a):
    hi = a.astype(BF16)
    return hi, (a - hi.astype(F32)).astype(BF16)


def mm(a, b):
    return jnp.dot(a, b, preferred_element_type=F32)


def mm_nt(a, b):
    return lax.dot_general(a, b, (((1,), (1,)), ((), ())), preferred_element_type=F32)


def mm3(a, b):
    return mm(a[0], b[0]) + mm(a[1], b[0]) + mm(a[0], b[1])


def left_pair(a):
    high, low = split(a)
    upper = jnp.concatenate([high, high], axis=1)
    lower = jnp.concatenate([low, jnp.zeros_like(low)], axis=1)
    return jnp.concatenate([upper, lower], axis=0)


def right_pair(a):
    high, low = split(a)
    none = jnp.zeros((128 - a.shape[0], a.shape[1]), BF16)
    return jnp.concatenate([high, none, low, none], axis=0)


def mm_pair(left, right):
    both = mm(left, right)
    half = left.shape[0] // 2
    return both[:half] + both[half:]


def iota(shape, dim):
    return lax.broadcasted_iota(jnp.int32, shape, dim)


def eliminate(target, column, row, first):
    if first < 7:
        return target - column * row
    lower = target[8:] - column[8:] * row
    return jnp.concatenate([target[:8], lower], axis=0)


def prepare_kernel(x_ref, off_ref, high_ref, low_ref, window_ref, xbuf, off, sems, off_sem):
    count = sems.shape[0]
    size = ROWS // count
    fetch = pltpu.make_async_copy(off_ref, off, off_sem)
    fetch.start()
    copies = []
    for j in range(count):
        rows = pl.ds(j * size, size)
        copies.append(pltpu.make_async_copy(x_ref.at[rows], xbuf.at[rows], sems.at[j]))
        copies[-1].start()
    fetch.wait()
    sweep = iota((SWEEPS, ROWS), 0)
    offset = jnp.zeros((SWEEPS, ROWS), jnp.int32)
    for s in range(SWEEPS):
        offset = jnp.where(sweep == s, off[s], offset)
    window = jnp.right_shift(iota((SWEEPS, ROWS), 1) - offset, 6)
    window_ref[...] = jnp.where((window < 0) & (lax.axis_index("row") == 0), -2, window)
    for j in range(count):
        copies[j].wait()
        rows = slice(j * size, (j + 1) * size)
        high, low = split(xbuf[rows])
        high_ref[rows] = high
        low_ref[rows] = low


def reflector_rows(vector_refs, window_ref):
    vectors = [ref[...] for ref in vector_refs]
    if len(vectors) == 2:
        first = lax.axis_index("col") == 0
        own, other = vectors
        vectors = [jnp.where(first, own, other), jnp.where(first, other, own)]
    refl = jnp.concatenate(vectors, axis=0)
    window = window_ref[...]
    return jnp.concatenate(
        [jnp.where(window == k, refl, 0.0) for k in range(-1, WINDOWS)], axis=0
    )


def halves_of(vt):
    return vt[:BAND, :HALF], vt[-BAND:, HALF:]


def project_kernel(chunk, inputs, *refs):
    window_ref, high_ref, low_ref = refs[inputs : inputs + 3]
    sums_ref, beside_ref, across_ref, down_ref, up_ref, solve_ref = refs[inputs + 3 :]
    columns = high_ref.shape[1]
    is_even = lax.rem(lax.axis_index("row"), 2) == 0
    vt = reflector_rows(refs[:inputs], window_ref)

    def send(cut, down, up):
        down_ref[:, cut] = down
        up_ref[:, cut] = up
        beside_ref[:, cut] = jnp.where(is_even, up[:8], down[:8])
        across_ref[:, cut] = jnp.where(is_even, down[:8], up[:8])

    tau = 2.0 / jnp.sum(vt[SWEEPS:-SWEEPS] * vt[SWEEPS:-SWEEPS], axis=1, keepdims=True)
    halves = [split(v) for v in halves_of(vt)]
    grams = [mm_nt(h, h) + mm_nt(l, h) + mm_nt(h, l) for h, l in halves]

    strict = iota((SWEEPS, BAND), 1) % SWEEPS < iota((SWEEPS, BAND), 0)

    def gram(k, shift):
        row = (k + 1) * SWEEPS
        if k < 3:
            return grams[0][row : row + SWEEPS], (k + 1 + shift) * SWEEPS
        row -= 4 * SWEEPS
        return grams[1][row : row + SWEEPS], (k - 3 + shift) * SWEEPS

    def strict_columns(k, shift, scale):
        block, base = gram(k, shift)
        if k == 3 and shift == 0:
            both = grams[0][4 * SWEEPS :, 4 * SWEEPS :] + grams[1][:SWEEPS, :SWEEPS]
            block, base = both, 0
        block = jnp.where(strict[:, : block.shape[1]], block, 0.0)
        if scale is not None:
            block = block * scale
        return lambda s: block[:, base + s : base + s + 1]

    tall = [jnp.concatenate([h, l], axis=0) for h, l in halves]
    chunks = columns // chunk

    def project(j):
        cut = slice(j * chunk, (j + 1) * chunk)
        sums = []
        for part in range(2):
            rows = slice(part * HALF, (part + 1) * HALF)
            both = mm(tall[part], high_ref[rows, cut])
            sums.append(both[:BAND] + both[BAND:] + mm(halves[part][0], low_ref[rows, cut]))
        shared = sums[0][-SWEEPS:] + sums[1][:SWEEPS]
        sums_ref[: 3 * SWEEPS, cut] = sums[0][SWEEPS:-SWEEPS]
        sums_ref[3 * SWEEPS : 4 * SWEEPS, cut] = shared
        sums_ref[4 * SWEEPS :, cut] = sums[1][SWEEPS:-SWEEPS]
        down_ref[:, cut] = sums[0][:SWEEPS]
        up_ref[:, cut] = sums[1][-SWEEPS:]

    lane = iota((SWEEPS, 128), 1)
    sub = iota((SWEEPS, 128), 0)
    state = []
    inner, outer = [], []
    for k in range(WINDOWS):
        here = lane == sub + k * SWEEPS
        if k < WINDOWS - 1:
            scale = tau[k * SWEEPS : (k + 1) * SWEEPS]
            state.append(jnp.where(here, scale, 0.0))
            inner.append(strict_columns(k, 0, scale))
            outer.append(strict_columns(k, 1, scale))
        else:
            state.append(jnp.where(here, 1.0, 0.0))
    leave = jnp.zeros((SWEEPS, 128), F32)
    leaving = strict_columns(-1, 1, None)
    for s in range(SWEEPS - 1):
        for j in range(s * chunks // (SWEEPS - 1), (s + 1) * chunks // (SWEEPS - 1)):
            project(j)
        rows = [state[k][s : s + 1] for k in range(WINDOWS)]
        for k in range(WINDOWS - 1):
            state[k] = eliminate(state[k], inner[k](s), rows[k], s)
            state[k] = eliminate(state[k], outer[k](s), rows[k + 1], s)
        leave = eliminate(leave, leaving(s), rows[0], s)

    solve = jnp.concatenate(state[: WINDOWS - 1], axis=0)
    solve_ref[...] = solve
    pass_on = left_pair(leave)

    bottom = jnp.concatenate([grams[0][:SWEEPS], jnp.zeros((SWEEPS, 128 - BAND), F32)], axis=1)
    top = jnp.concatenate([grams[1][-SWEEPS:], jnp.zeros((SWEEPS, 128 - BAND), F32)], axis=1)
    top = jnp.where(lane < SWEEPS, pltpu.roll(top, 128 - 4 * SWEEPS, 1), 0.0)
    response = pltpu.roll(leave, 2 * SWEEPS, 1)
    side = jnp.where(lane < SWEEPS, bottom, jnp.where(lane < 2 * SWEEPS, response, 0.0))
    extra = slice(columns, columns + EXTRA)
    down_ref[:, extra] = side
    up_ref[:, extra] = top

    def fold(a):
        return jnp.where(lane[:8] < SWEEPS, a[:8], pltpu.roll(a[8:], 2 * SWEEPS, 1))

    bottom, top = fold(bottom), fold(top)
    beside_ref[:, extra] = jnp.where(is_even, top, bottom)
    across_ref[:, extra] = jnp.where(is_even, bottom, top)

    for j in range(chunks):
        cut = slice(j * chunk, (j + 1) * chunk)
        leaving = mm_pair(pass_on, right_pair(sums_ref[:, cut]))
        send(cut, down_ref[:, cut] + leaving, up_ref[:, cut])


def bands_of(first, local, last):
    return (
        jnp.concatenate([first, local[: 4 * SWEEPS]], axis=0),
        jnp.concatenate([local[3 * SWEEPS :], last], axis=0),
    )


def stack(a):
    high, low = split(a)
    return jnp.concatenate([high, high, low], axis=0)


def straddling(gram, base):
    size = gram.shape[0]
    lane, sub = iota((size, 128), 1), iota((size, 128), 0)
    squares = jnp.sum(jnp.where(sub == lane, gram, 0.0), axis=1, keepdims=True)
    tau = jnp.where(squares > 0.0, 2.0 / squares, 0.0)
    strict = jnp.where(lane < sub, gram, 0.0) * tau
    return tau, strict, jnp.where(lane == sub + base, tau, 0.0)


def complete_kernel(parity, down_ref, up_ref, got_ref, *refs):
    send_ref = refs[-1]
    columns = down_ref.shape[1] - EXTRA
    row, count = lax.axis_index("row"), lax.axis_size("row")
    ours = lax.rem(row, 2) == parity

    def got(cut):
        return jnp.where(row < count - 1, got_ref[:, cut], 0.0)

    side = slice(columns, columns + EXTRA)
    own_side = down_ref[8:, side]
    _, strict, solve = straddling(up_ref[:8, side] + got(side), 0)
    carry = jnp.zeros((8, 128), F32)
    for s in range(8):
        row_s = solve[s : s + 1]
        carry = carry + own_side[:, SWEEPS + s : SWEEPS + s + 1] * row_s
        if s < 7:
            solve = solve - strict[:, s : s + 1] * row_s
    for place in range(0, columns, 128):
        cut = slice(place, place + 128)
        down = down_ref[8:, cut]
        below = up_ref[:8, cut] + got(cut)
        for s in range(8):
            down = down + carry[:, s : s + 1] * below[s : s + 1]
        send_ref[:, cut] = jnp.where(ours, down, up_ref[8:, cut])
    if send_ref.shape[1] > columns:
        send_ref[:, side] = jnp.zeros((8, EXTRA), F32)


def local_part(cut, high_ref, low_ref, sums_ref, cols_ref, solve):
    coeff = mm_pair(solve, right_pair(sums_ref[:, cut]))
    none = jnp.zeros((SWEEPS, coeff.shape[1]), F32)
    for part, band in enumerate(bands_of(none, coeff, none)):
        rows = slice(part * HALF, (part + 1) * HALF)
        slab = high_ref[rows, cut].astype(F32) + low_ref[rows, cut].astype(F32)
        yield rows, slab - mm(cols_ref[rows, :], stack(band))


def subtract_inside(chunk, begin, high_ref, low_ref, sums_ref, cols_ref, solve, inner_ref):
    solve = left_pair(solve)
    for place in range(0, inner_ref.shape[1], chunk):
        cut = slice(begin + place, begin + place + chunk)
        for rows, inner in local_part(cut, high_ref, low_ref, sums_ref, cols_ref, solve):
            inner_ref[rows, place : place + chunk] = inner


def inside_kernel(chunk, inputs, *refs):
    window_ref, high_ref, low_ref, sums_ref, solve_ref, _ = refs[inputs : inputs + 6]
    inner_ref, ends_ref, cols_ref = refs[inputs + 6 :]
    for part, v in enumerate(halves_of(reflector_rows(refs[:inputs], window_ref))):
        high, low = (a.astype(F32) for a in split(v))
        tall = jnp.concatenate([high, low, high], axis=0)
        cols_ref[part * HALF : (part + 1) * HALF, :] = jnp.transpose(tall).astype(BF16)
    solve = solve_ref[...]
    lane = iota((LOCAL, 128), 1)
    spread = jnp.zeros((LOCAL, 128), F32)
    for group in range(3):
        begin = 2 * SWEEPS * group + SWEEPS
        moved = pltpu.roll(solve, SWEEPS + begin, 1)
        spread = jnp.where((lane >= begin) & (lane < begin + SWEEPS), moved, spread)
    lane, sub = iota((SWEEPS, 128), 1), iota((SWEEPS, 128), 0)
    used = lane < 6 * SWEEPS
    first = jnp.where((lane % (2 * SWEEPS) == sub) & used, 1.0, 0.0)
    last = jnp.where((lane % (2 * SWEEPS) == sub + SWEEPS) & used, 1.0, 0.0)
    for part, band in enumerate(bands_of(first, spread, last)):
        rows = slice(part * HALF, (part + 1) * HALF)
        high, low = split(mm(cols_ref[rows, :], stack(band)))
        group = iota((HALF, 128), 1) // (2 * SWEEPS)
        ends_ref[rows, :] = jnp.where(group == 1, low.astype(F32), high.astype(F32)).astype(BF16)

    subtract_inside(chunk, 0, high_ref, low_ref, sums_ref, cols_ref, solve, inner_ref)


def from_neighbours(across, beside):
    row, count = lax.axis_index("row"), lax.axis_size("row")
    is_even = lax.rem(row, 2) == 0
    across = jnp.where((row > 0) & (row < count - 1), across, 0.0)
    return jnp.where(is_even, beside, across), jnp.where(is_even, across, beside)


def inside_more_kernel(chunk, begin, *refs):
    high_ref, low_ref, sums_ref, solve_ref, cols_ref = refs[:5]
    across_ref, beside_ref, down_ref, up_ref, ends_ref, inner_ref, effect_ref = refs[5:]
    extra = slice(down_ref.shape[1] - EXTRA, down_ref.shape[1])

    def unfold(a):
        return jnp.concatenate([a, pltpu.roll(a, 128 - 2 * SWEEPS, 1)], axis=0)

    below, above = from_neighbours(across_ref[:, extra], beside_ref[:, extra])
    own_side = down_ref[:, extra]
    _, n7, c7 = straddling(up_ref[:, extra] + unfold(below), 0)
    tau1, n1, c1 = straddling(unfold(above) + own_side, SWEEPS)
    e1 = own_side * tau1
    for s in range(SWEEPS - 1):
        row7, row1 = c7[s : s + 1], c1[s : s + 1]
        c7 = eliminate(c7, n7[:, s : s + 1], row7, s)
        c1 = eliminate(c1, n1[:, s : s + 1], row1, s)
        c1 = eliminate(c1, -e1[:, SWEEPS + s : SWEEPS + s + 1], row7, s)
    join = jnp.concatenate([c1, c7], axis=0)
    join = join + pltpu.roll(join, 2 * SWEEPS, 1) + pltpu.roll(join, 4 * SWEEPS, 1)
    high, low = split(mm(ends_ref[:, : 6 * SWEEPS], stack(join)))
    group = iota(high.shape, 1) // (2 * SWEEPS)
    effect = jnp.where(group == 1, low.astype(F32), high.astype(F32))
    effect_ref[...] = effect.astype(BF16)
    subtract_inside(chunk, begin, high_ref, low_ref, sums_ref, cols_ref, solve_ref[...], inner_ref)


def finish_kernel(chunk, *refs):
    first_across, last_across, first_beside, last_beside = refs[:4]
    down_ref, up_ref, effect_ref, high_ref, low_ref, sums_ref, cols_ref, solve_ref = refs[4:12]
    inner_refs, (out_ref, obuf, sems) = refs[12:14], refs[14:]
    columns = high_ref.shape[1]
    effect = effect_ref[:, : 6 * SWEEPS]
    solve = left_pair(solve_ref[...])

    def messages(cut):
        across = jnp.concatenate([first_across[:, cut], last_across[:, cut]], axis=0)
        beside = jnp.concatenate([first_beside[:, cut], last_beside[:, cut]], axis=0)
        below, above = from_neighbours(across, beside)
        return stack(jnp.concatenate([up_ref[:, cut] + below, down_ref[:, cut] + above], axis=0))

    stores = []
    pieces = []
    for ref in inner_refs:
        for place in range(0, ref.shape[1], chunk):
            pieces.append((ref, place))
    for j in range(columns // chunk):
        cut = slice(j * chunk, (j + 1) * chunk)
        coeff = messages(cut)
        if j < len(pieces):
            ref, place = pieces[j]
            obuf[:, cut] = ref[:, place : place + chunk] - mm(effect, coeff)
        else:
            for rows, inner in local_part(cut, high_ref, low_ref, sums_ref, cols_ref, solve):
                obuf[rows, cut] = inner - mm(effect[rows], coeff)
        cut = pl.ds(j * chunk, chunk)
        stores.append(pltpu.make_async_copy(obuf.at[:, cut], out_ref.at[:, cut], sems.at[j]))
        stores[-1].start()
    for store in stores:
        store.wait()


def in_hbm(a):
    return pltpu.with_memory_space_constraint(a, pltpu.HBM)


def local(eig_slab, reflectors, row_offsets):
    rows, columns = eig_slab.shape
    assert rows == ROWS and columns % 256 == 0
    chunk = 256 if columns % 512 == 0 else 128
    chunks = columns // chunk
    wide = 2 * chunk if chunks % 8 == 0 else chunk
    count = lax.axis_size("row")
    groups = lax.axis_size("col")
    vmem = pl.BlockSpec(memory_space=pltpu.VMEM)
    hbm = pl.BlockSpec(memory_space=pltpu.HBM)
    params = pltpu.CompilerParams(vmem_limit_bytes=16 * 1024 * 1024)
    shape = jax.ShapeDtypeStruct
    slab_bytes = rows * columns * 4

    def cost(passes, flops):
        return pl.CostEstimate(flops=flops, bytes_accessed=passes * slab_bytes, transcendentals=0)

    if groups == 2:
        vectors = (reflectors, lax.ppermute(reflectors, "col", [(0, 1), (1, 0)]))
    elif groups == 1:
        vectors = (reflectors,)
    else:
        vectors = (lax.all_gather(reflectors, "col", axis=0, tiled=True),)

    high, low, window = pl.pallas_call(
        prepare_kernel,
        out_shape=(
            shape((rows, columns), BF16),
            shape((rows, columns), BF16),
            shape((SWEEPS, rows), jnp.int32),
        ),
        in_specs=[hbm, hbm],
        out_specs=(vmem,) * 3,
        scratch_shapes=[
            pltpu.VMEM((rows, columns), F32),
            pltpu.SMEM((SWEEPS,), jnp.int32),
            pltpu.SemaphoreType.DMA((8,)),
            pltpu.SemaphoreType.DMA(()),
        ],
        compiler_params=params,
        cost_estimate=cost(2, 0),
        name="prepare",
    )(in_hbm(eig_slab), in_hbm(row_offsets))

    own = shape((SWEEPS, columns + EXTRA), F32)
    eight = shape((8, columns + EXTRA), F32)
    sums, beside, across, down, up, solve = pl.pallas_call(
        functools.partial(project_kernel, wide, len(vectors)),
        out_shape=(
            shape((LOCAL, columns), F32),
            eight,
            eight,
            own,
            own,
            shape((LOCAL, 128), F32),
        ),
        in_specs=[vmem] * (len(vectors) + 3),
        out_specs=(vmem,) * 6,
        compiler_params=params,
        cost_estimate=cost(2, rows * columns * 240),
        name="project",
    )(*vectors, window, high, low)

    pairs = [(i, i + 1) for i in range(0, count, 2)]
    on_chip = pairs + [(j, i) for i, j in pairs]
    pairs = [
        (i * groups + c, (i + 1) * groups + c)
        for i in range(1, count - 1, 2)
        for c in range(groups)
    ]
    pairs += [
        (i * groups + c, i * groups + c + 1)
        for i in (0, count - 1)
        for c in range(0, groups - 1, 2)
    ]
    over_chips = pairs + [(j, i) for i, j in pairs]

    got_beside = lax.ppermute(beside, "row", on_chip)
    got_across = lax.ppermute(across, ("row", "col"), over_chips)
    late = pl.pallas_call(
        functools.partial(complete_kernel, 0),
        out_shape=eight,
        in_specs=[vmem] * 3,
        out_specs=vmem,
        compiler_params=params,
        name="complete_even",
    )(down, up, got_beside)
    got_late = lax.ppermute(late, ("row", "col"), over_chips)

    inside_first = (chunks + 1) // 2 * chunk
    inside_next = (chunks + 2) // 4 * chunk
    inner, ends, cols = pl.pallas_call(
        functools.partial(inside_kernel, wide, len(vectors)),
        out_shape=(shape((rows, inside_first), F32), shape((rows, 128), BF16), shape((rows, 3 * BAND), BF16)),
        in_specs=[vmem] * (len(vectors) + 6),
        out_specs=(vmem,) * 3,
        compiler_params=params,
        cost_estimate=cost(2, rows * columns * 240),
        name="inside",
    )(*vectors, window, high, low, sums, solve, late)

    latest = pl.pallas_call(
        functools.partial(complete_kernel, 1),
        out_shape=shape((8, columns), F32),
        in_specs=[vmem] * 4,
        out_specs=vmem,
        compiler_params=params,
        name="complete_odd",
    )(down, up, got_across, ends)
    got_latest = lax.ppermute(latest, "row", on_chip)

    more, effect = pl.pallas_call(
        functools.partial(inside_more_kernel, wide, inside_first),
        out_shape=(shape((rows, inside_next), F32), shape((rows, 128), BF16)),
        in_specs=[vmem] * 10,
        out_specs=(vmem,) * 2,
        compiler_params=params,
        cost_estimate=cost(2, rows * columns * 240),
        name="inside_more",
    )(high, low, sums, solve, cols, got_across, got_beside, down, up, ends)

    return pl.pallas_call(
        functools.partial(finish_kernel, wide),
        out_shape=shape((rows, columns), F32),
        in_specs=[vmem] * 14,
        out_specs=hbm,
        scratch_shapes=[
            pltpu.VMEM((rows, columns), F32),
            pltpu.SemaphoreType.DMA((chunks,)),
        ],
        compiler_params=params,
        cost_estimate=cost(2, rows * columns * 200),
        name="finish",
    )(got_across, got_late, got_beside, got_latest, down, up, effect, high, low, sums, cols, solve, inner, more)


def solution(mesh):
    placed = (P("row", "col"), P("col", "row"), P())
    return jax.shard_map(
        local, mesh=mesh, in_specs=placed, out_specs=P("row", "col"), check_vma=False
    )
```
